32 devices in a mesh: pole: 2 (over y), row: 4 (over x, core), col: 4 (over z).
Axes of the slice: x: 2, y: 2, z: 4, core: 2. Of those that a mesh axis runs over, the one named last changes fastest.
Arguments:
- inverse: bfloat16 [2, 2, 8192, 8192], P('pole', None, None, ('row', 'col')), may hold values from -0.0625 to 0.0625
- factor: bfloat16 [2, 2, 8192, 768], P('pole', None, ('row', 'col')), may hold values from -1 to 1
- diag_inverse: bfloat16 [2, 2, 768, 256], P('pole', None, ('row', 'col')), may hold values from -6 to 6
- widths: int32 [3], replicated, may hold values from 1 to 256, 512 in all
- pattern: int32 [32, 3], replicated, may hold values 0 or 1
- owner: int32 [16], replicated, may hold values from 0 to 15, each once
- assign: int32 [2], P('pole'), may hold values from 0 to 19
- pole_weights: float32 [20, 2], replicated, may hold values from -4 to 4
Outputs:
- rho_panel: float32 [8192, 768], P(('row', 'col'))
- rho_diag: float32 [768, 256], P(('row', 'col'))
The draws below stay inside these ranges and needn't reach their ends.
Inputs may be any that keep to these rules, and one draw needn't show every extreme that they name: The widths sum to 512 and the largest is exactly 256. `owner`: each piece number appears once.
All inputs are finite; a program needn't handle non-finite values.
Results may differ from the reference program's by a relative error of at most 0.0027.
Values may be sent and summed in bfloat16 or wider, within the bound.
A program may use at most 192 MiB of HBM per device.

```python
import math
import jax
import jax.numpy as jnp
import numpy as np
from jax import lax

B = 256
NA = 32
NK = 3
NPOLE = 20
P_SIZE = 2
N = 8192
M = 768
G = 16
N_ROW = 4
N_COL = 4


def touch_ends(values, own_key, smallest, largest):
    index_at = [jax.random.randint(jax.random.fold_in(own_key, axis), (), 0, length) for axis, length in enumerate(values.shape)]
    widest = values.shape.index(max(values.shape))
    neighbour = index_at[:widest] + [(index_at[widest] + 1) % values.shape[widest]] + index_at[widest + 1:]
    return values.at[tuple(index_at)].set(smallest).at[tuple(neighbour)].set(largest)


def shard_levels(own_key, shape, shards, smallest, largest):
    def one(axis_at, shards_of):
        heights = jax.random.uniform(jax.random.fold_in(jax.random.fold_in(own_key, 6), axis_at), (shards_of,), jnp.float32, smallest / len(shards), largest / len(shards))
        return jnp.repeat(jnp.exp(heights), shape[axis_at] // shards_of).reshape((-1,) + (1,) * (len(shape) - axis_at - 1))

    level = one(*shards[0])
    for cut in shards[1:]:
        level = level * one(*cut)
    return level


def profile(number_of, total, reach, slope):
    weights = [(1 << 20) // math.isqrt(grade ** slope) + 1 for grade in range(2, number_of + 1)]
    rest, given = total - reach - (number_of - 1), [1] * (number_of - 1)
    while rest > 0:
        free = [i for i in range(number_of - 1) if given[i] < reach]
        mass, budget = sum([weights[i] for i in free]), rest
        for i in free:
            extra = min(reach - given[i], max(1, budget * weights[i] // mass), rest)
            given[i] = given[i] + extra
            rest = rest - extra
    return np.array([reach] + given)


def uneven_parts(rng, number_of, total, most, skew):
    if number_of == 2:
        one = jax.random.randint(rng, (), max(1, total - most), min(most, total - 1) + 1)
        return jnp.stack([one, total - one])
    lengths = jnp.asarray(profile(number_of, total, most, skew), jnp.int32)
    twos = (number_of - 1) // 2
    donor, receiver = lengths[1:1 + 2 * twos:2], lengths[2:2 + 2 * twos:2]
    margin = jnp.minimum(donor - 1, most - receiver)
    passed = jax.random.randint(jax.random.fold_in(rng, 1), (twos,), 0, 1 << 20) % (margin + 1)
    lengths = lengths.at[1:1 + 2 * twos:2].set(donor - passed).at[2:2 + 2 * twos:2].set(receiver + passed)
    return lengths[jax.random.permutation(jax.random.fold_in(rng, 2), number_of)]


def centred(own_key, extent, deviation, reach, split=(), kind=jnp.bfloat16):
    array = jax.random.normal(own_key, extent, jnp.float32) * deviation
    if len(split) > 0:
        array = shard_levels(own_key, extent, split, -0.22, 0.18) * array
    return jnp.clip(array, min=-reach, max=reach).astype(kind)


def setup_inputs(seed: int = 0) -> dict:
    splits = jax.random.split(jax.random.key(seed), 9)
    return {
        "inverse": centred(splits[0], (P_SIZE, 2, N, N), (NA * B) ** -0.5, 0.0625, ((0, 2), (3, 16))),
        "factor": centred(splits[1], (P_SIZE, 2, N, M), 0.15, 1.0, ((0, 2), (2, 16))),
        "diag_inverse": centred(splits[2], (P_SIZE, 2, M, B), 1.0, 6.0, ((0, 2), (2, 16))),
        "widths": uneven_parts(splits[3], NK, 2 * NK * B // 3, B, 1).astype(jnp.int32),
        "pattern": touch_ends((jax.random.randint(splits[4], (NA, NK), 0, 3) < 2).astype(jnp.int32), jax.random.fold_in(splits[4], 1), 0, 1),
        "owner": jax.random.permutation(splits[5], G).astype(jnp.int32),
        "assign": jax.random.randint(splits[6], (P_SIZE,), 0, NPOLE).astype(jnp.int32),
        "pole_weights": centred(splits[7], (NPOLE, 2), 1.0, 4.0, (), jnp.float32),
    }


def plain_dot(left, right):
    return jnp.dot(left, right, preferred_element_type=jnp.float32)


def reference(inverse, factor, diag_inverse, widths, pattern, owner, assign, pole_weights):
    grid_count = N_ROW * N_COL
    total_rows = NA * B
    total_cols = NK * B
    piece_rows = total_rows // grid_count
    row_block = (jnp.arange(total_rows) // B).astype(jnp.int32)
    col_block = (jnp.arange(total_cols) // B).astype(jnp.int32)
    col_pos = (jnp.arange(total_cols) % B).astype(jnp.int32)
    col_live = (col_pos < widths[col_block]).astype(jnp.int32)
    keep = pattern[row_block][:, col_block] * col_live[None, :]
    masked = factor * keep.astype(jnp.bfloat16)[None, None]
    weights = pole_weights[assign]

    def one_pole(inputs):
        inv, panel, dinv, weight = inputs
        sum_real = plain_dot(inv[0].T, panel[0]) - plain_dot(inv[1].T, panel[1])
        sum_imag = plain_dot(inv[0].T, panel[1]) + plain_dot(inv[1].T, panel[0])
        x_real = -sum_real
        x_imag = -sum_imag
        panel_density = weight[0] * x_imag + weight[1] * x_real
        x_bf = jnp.stack([x_real, x_imag]).astype(jnp.bfloat16)
        own = panel.reshape(2, grid_count, piece_rows, total_cols)[:, owner].reshape(2, total_rows, total_cols)
        own_blocks = own.reshape(2, total_rows, NK, B).astype(jnp.float32)
        x_blocks = x_bf.reshape(2, total_rows, NK, B).astype(jnp.float32)
        part_real = jnp.einsum("nka,nkb->kab", own_blocks[0], x_blocks[0]) - jnp.einsum("nka,nkb->kab", own_blocks[1], x_blocks[1])
        part_imag = jnp.einsum("nka,nkb->kab", own_blocks[0], x_blocks[1]) + jnp.einsum("nka,nkb->kab", own_blocks[1], x_blocks[0])
        diag_real = dinv[0].astype(jnp.float32) - part_real.reshape(total_cols, B)
        diag_imag = dinv[1].astype(jnp.float32) - part_imag.reshape(total_cols, B)
        diag_density = weight[0] * diag_imag + weight[1] * diag_real
        return panel_density, diag_density

    panels, diags = lax.map(one_pole, (inverse, masked, diag_inverse, weights))
    return jnp.sum(panels, axis=0), jnp.sum(diags, axis=0)
```

```python
import functools

import jax
import jax.numpy as jnp
from jax import lax
from jax.experimental import pallas as pl
from jax.experimental.pallas import tpu as pltpu
from jax.sharding import PartitionSpec as P

F32 = jnp.float32
BF16 = jnp.bfloat16
MESH = pl.DeviceIdType.MESH


def dot(left, right):
    return jnp.dot(left, right, preferred_element_type=F32)


def dot_nt(left, right):
    return lax.dot_general(left, right, (((1,), (1,)), ((), ())), preferred_element_type=F32)


def kernel(
    dims,
    piece_ref,
    inv_ref,
    place_ref,
    weight_ref,
    own_ref,
    dinv_ref,
    panel_ref,
    diag_ref,
    pieces,
    inv,
    acc,
    shares,
    xe,
    le,
    gram,
    half,
    half_sum,
    parts,
    totals,
    inv_sem,
    recv,
    sz,
    sx,
    sc,
    ys,
    yr,
    d1s,
    d1r,
    d2s,
    d2r,
    d3s,
    d3r,
):
    chunks, zs, poles, width, blocks_k, block, db = dims
    pole = lax.axis_index("pole")
    row = lax.axis_index("row")
    z = lax.axis_index("col")
    hi = row // 2
    lo = row % 2
    sibling = hi * 2 + (1 - lo)
    across = (1 - hi) * 2 + lo

    def at(h, l, zz):
        return (h * 2 + l) * zs + zz

    me = at(hi, lo, z)
    mine = hi * zs + z

    barrier = pltpu.get_barrier_semaphore()
    pl.semaphore_signal(
        barrier, inc=1, device_id=(pole, sibling, z), device_id_type=MESH
    )

    @pl.loop(0, 2 * zs)
    def _(j):
        @pl.when(j != mine)
        def _():
            pl.semaphore_signal(
                barrier,
                inc=1,
                device_id=(pole, (j // zs) * 2 + lo, j % zs),
                device_id_type=MESH,
            )

    @pl.loop(0, poles)
    def _(p):
        @pl.when(p != pole)
        def _():
            pl.semaphore_signal(
                barrier, inc=1, device_id=(p, row, z), device_id_type=MESH
            )

    load = pltpu.make_async_copy(inv_ref, inv, inv_sem)
    load.start()
    pieces[:, pl.ds(me, 1)] = piece_ref[...][:, None]
    pl.semaphore_wait(barrier, 1 + (2 * zs - 1) + (poles - 1))

    def send(c, q, send_sem, to_row, to_col):
        return pltpu.make_async_remote_copy(
            src_ref=pieces.at[c, q],
            dst_ref=pieces.at[c, q],
            send_sem=send_sem,
            recv_sem=recv.at[c, q],
            device_id=(pole, to_row, to_col),
            device_id_type=MESH,
        )

    def up(c, zz):
        return send(c, at(hi, lo, zz), sz.at[c, zz, 1], row, z + 1)

    def down(c, zz):
        return send(c, at(hi, lo, zz), sz.at[c, zz, 0], row, z - 1)

    def cross(c, zz):
        return send(c, at(hi, lo, zz), sx.at[c, zz], across, z)

    def over(c, h, zz):
        return send(c, at(h, lo, zz), sc.at[c, h, zz], sibling, z)

    def arrived(c, q):
        send(c, q, sx.at[0, 0], across, z).wait_recv()

    def goes_up(zz):
        return (zz <= z) & (z < zs - 1)

    def goes_down(zz):
        return (zz >= z) & (z > 0)

    def forward(c, zz):
        cross(c, zz).start()

        @pl.when(goes_up(zz))
        def _():
            up(c, zz).start()

        @pl.when(goes_down(zz))
        def _():
            down(c, zz).start()

        over(c, hi, zz).start()

    @pl.loop(0, chunks)
    def _(c):
        forward(c, z)

    acc[...] = jnp.zeros_like(acc)
    xe[...] = jnp.zeros_like(xe)
    le[...] = jnp.zeros_like(le)
    panel_ref[...] = jnp.zeros_like(panel_ref)
    load.wait()

    def compute(c, q):
        lt = pieces[c, q]
        u = dot(lt, inv[0, q])
        v = dot(lt, inv[1, q])
        acc[c, :width] += u[:width] - v[width:]
        acc[c, width:] += u[width:] + v[:width]

    def by_distance(visit, first):
        @pl.loop(first, 2 * zs)
        def _(j):
            s = j // 2
            zz = jnp.where(j % 2 == 0, z - s, z + s)

            @pl.when((zz >= 0) & (zz < zs) & (j != 1))
            def _():
                visit(zz)

    def along(c):
        compute(c, me)

        def visit(zz):
            arrived(c, at(hi, lo, zz))
            forward(c, zz)
            compute(c, at(hi, lo, zz))

        by_distance(visit, 2)

    def crossed(c):
        def visit(zz):
            arrived(c, at(1 - hi, lo, zz))
            over(c, 1 - hi, zz).start()
            compute(c, at(1 - hi, lo, zz))

        by_distance(visit, 0)

    def from_sibling(c, h):
        def visit(zz):
            arrived(c, at(h, 1 - lo, zz))
            compute(c, at(h, 1 - lo, zz))

        by_distance(visit, 0)

    def share(c, p):
        return pltpu.make_async_remote_copy(
            src_ref=shares.at[c, pole],
            dst_ref=shares.at[c, pole],
            send_sem=ys.at[c, p],
            recv_sem=yr.at[c, pole],
            device_id=(p, row, z),
            device_id_type=MESH,
        )

    def share_from(c, p):
        return pltpu.make_async_remote_copy(
            src_ref=shares.at[c, p],
            dst_ref=shares.at[c, p],
            send_sem=ys.at[c, p],
            recv_sem=yr.at[c, p],
            device_id=(p, row, z),
            device_id_type=MESH,
        )

    wr = weight_ref[0]
    wi = weight_ref[1]

    def others(visit):
        @pl.loop(0, poles)
        def _(p):
            @pl.when(p != pole)
            def _():
                visit(p)

    def finish(c):
        xr = -acc[c, :width]
        xi = -acc[c, width:]
        shares[c, pole] = wr * xi + wi * xr
        others(lambda p: share(c, p).start())
        place = place_ref[c]
        xe[0] += dot(place, xr.astype(BF16)).astype(BF16)
        xe[1] += dot(place, xi.astype(BF16)).astype(BF16)

    def receive(c):
        others(lambda p: share_from(c, p).wait_recv())
        total = shares[c, 0]
        for p in range(1, poles):
            total = total + shares[c, p]
        top = total.astype(BF16)
        rest = total - top.astype(F32)
        middle = rest.astype(BF16)
        low = (rest - middle.astype(F32)).astype(BF16)
        place = place_ref[c]
        panel_ref[...] += dot(place, top) + dot(place, middle) + dot(place, low)

    @pl.loop(0, chunks + 2)
    def _(t):
        @pl.when(t >= 2)
        def _():
            from_sibling(t - 2, 1 - hi)
            finish(t - 2)

        @pl.when(t < chunks)
        def _():
            along(t)

        @pl.when((t >= 1) & (t <= chunks))
        def _():
            from_sibling(t - 1, hi)
            crossed(t - 1)

    @pl.loop(0, chunks)
    def _(c):
        lt = pieces[c, own_ref[0]]
        place = place_ref[c]
        le[0] += dot(place, lt[:width]).astype(BF16)
        le[1] += dot(place, lt[width:]).astype(BF16)

    for k in range(blocks_k):
        rows = slice(k * block, (k + 1) * block)
        lr, li, xr, xi = le[0, rows], le[1, rows], xe[0, rows], xe[1, rows]
        real = dot_nt(lr, xr) - dot_nt(li, xi)
        imag = dot_nt(lr, xi) + dot_nt(li, xr)
        gram[rows] = wr * imag + wi * real

    span = zs * db

    def rows_of(h, l):
        return pl.ds(pl.multiple_of((h * 2 + l) * span, 8), span)

    halves = []
    for h in range(2):
        halves.append(
            pltpu.make_async_remote_copy(
                src_ref=gram.at[rows_of(h, 1 - lo)],
                dst_ref=half.at[h],
                send_sem=d1s.at[h],
                recv_sem=d1r.at[h],
                device_id=(pole, sibling, z),
                device_id_type=MESH,
            )
        )
        halves[h].start()

    @pl.loop(0, chunks - 1)
    def _(c):
        receive(c)

    for h in range(2):
        halves[h].wait_recv()
        half_sum[h] = (gram[rows_of(h, lo)] + half[h]).reshape(zs, db, block)

    def part(j):
        return pltpu.make_async_remote_copy(
            src_ref=half_sum.at[j // zs, j % zs],
            dst_ref=parts.at[mine],
            send_sem=d2s.at[j],
            recv_sem=d2r.at[mine],
            device_id=(pole, (j // zs) * 2 + lo, j % zs),
            device_id_type=MESH,
        )

    def part_from(j):
        return pltpu.make_async_remote_copy(
            src_ref=parts.at[j],
            dst_ref=parts.at[j],
            send_sem=d2s.at[j],
            recv_sem=d2r.at[j],
            device_id=(pole, (j // zs) * 2 + lo, j % zs),
            device_id_type=MESH,
        )

    def peers(visit):
        @pl.loop(0, 2 * zs)
        def _(j):
            @pl.when(j != mine)
            def _():
                visit(j)

    peers(lambda j: part(j).start())
    parts[mine] = half_sum[hi, z]
    receive(chunks - 1)
    peers(lambda j: part_from(j).wait_recv())
    total = parts[0]
    for j in range(1, 2 * zs):
        total = total + parts[j]
    totals[pole] = dinv_ref[...] - total

    def result(p, slot):
        return pltpu.make_async_remote_copy(
            src_ref=totals.at[slot],
            dst_ref=totals.at[slot],
            send_sem=d3s.at[p],
            recv_sem=d3r.at[slot],
            device_id=(p, row, z),
            device_id_type=MESH,
        )

    others(lambda p: result(p, pole).start())

    @pl.loop(0, chunks)
    def _(c):
        @pl.loop(0, zs)
        def _(zz):
            cross(c, zz).wait_send()
            over(c, 0, zz).wait_send()
            over(c, 1, zz).wait_send()

            @pl.when(goes_up(zz))
            def _():
                up(c, zz).wait_send()

            @pl.when(goes_down(zz))
            def _():
                down(c, zz).wait_send()

        others(lambda p: share(c, p).wait_send())

    for h in range(2):
        halves[h].wait_send()
    peers(lambda j: part(j).wait_send())
    others(lambda p: result(p, p).wait_recv())
    final = totals[0]
    for p in range(1, poles):
        final = final + totals[p]
    diag_ref[...] = final
    others(lambda p: result(p, pole).wait_send())


def local(inverse, factor, diag_inverse, widths, pattern, owner, assign, pole_weights):
    zs = lax.axis_size("col")
    poles = lax.axis_size("pole")
    rows_n = lax.axis_size("row")
    assert rows_n == 4
    devices = rows_n * zs
    device = lax.axis_index(("row", "col"))
    local_width = factor.shape[2]
    total_cols = factor.shape[3]
    db = diag_inverse.shape[2]
    block = diag_inverse.shape[3]
    blocks_k = total_cols // block
    live = 2 * total_cols // 3
    width = 128
    chunks = live // width

    col_ids = jnp.arange(total_cols, dtype=jnp.int32)
    col_block = col_ids // block
    col_pos = col_ids % block
    block_ids = jnp.arange(blocks_k, dtype=jnp.int32)
    same = col_block[:, None] == block_ids[None, :]
    before = block_ids[None, :] < col_block[:, None]
    col_width = jnp.sum(jnp.where(same, widths[None, :], 0), axis=1)
    col_start = jnp.sum(jnp.where(before, widths[None, :], 0), axis=1)
    target = jnp.where(col_pos < col_width, col_start + col_pos, -1)
    place = (target[:, None] == jnp.arange(live, dtype=jnp.int32)[None, :]).astype(BF16)

    row_block = (device * local_width + jnp.arange(local_width, dtype=jnp.int32)) // block
    row_onehot = (
        row_block[:, None] == jnp.arange(pattern.shape[0], dtype=jnp.int32)[None, :]
    ).astype(F32)
    row_mask = jnp.dot(row_onehot, pattern.astype(F32), precision=lax.Precision.HIGHEST)
    mask = jnp.repeat(row_mask, block, axis=1).astype(BF16)
    masked = factor[0] * mask[None]
    packed = lax.dot_general(
        place.reshape(total_cols, chunks, width),
        masked,
        (((0,), (2,)), ((), ())),
        preferred_element_type=F32,
    ).astype(BF16)
    packed = packed.transpose(0, 2, 1, 3).reshape(chunks, 2 * width, local_width)

    pole_onehot = assign[0] == jnp.arange(pole_weights.shape[0], dtype=jnp.int32)
    weight = jnp.sum(jnp.where(pole_onehot[:, None], pole_weights, 0.0), axis=0)
    own = jnp.sum(jnp.where(jnp.arange(devices, dtype=jnp.int32) == device, owner, 0))
    inverse_diag = diag_inverse[0].astype(F32)
    dinv = weight[0] * inverse_diag[1] + weight[1] * inverse_diag[0]
    places = place.reshape(total_cols, chunks, width).transpose(1, 0, 2)

    dims = (chunks, zs, poles, width, blocks_k, block, db)
    vmem = pl.BlockSpec(memory_space=pltpu.VMEM)
    smem = pl.BlockSpec(memory_space=pltpu.SMEM)
    dma = pltpu.SemaphoreType.DMA
    panel, diag = pl.pallas_call(
        functools.partial(kernel, dims),
        out_shape=(
            jax.ShapeDtypeStruct((total_cols, local_width), F32),
            jax.ShapeDtypeStruct((db, block), F32),
        ),
        in_specs=[vmem, pl.BlockSpec(memory_space=pl.ANY), vmem, smem, smem, vmem],
        out_specs=(vmem, vmem),
        scratch_shapes=[
            pltpu.VMEM((chunks, devices, 2 * width, local_width), BF16),
            pltpu.VMEM((2, devices, local_width, local_width), BF16),
            pltpu.VMEM((chunks, 2 * width, local_width), F32),
            pltpu.VMEM((chunks, poles, width, local_width), F32),
            pltpu.VMEM((2, total_cols, local_width), BF16),
            pltpu.VMEM((2, total_cols, local_width), BF16),
            pltpu.VMEM((total_cols, block), F32),
            pltpu.VMEM((2, zs * db, block), F32),
            pltpu.VMEM((2, zs, db, block), F32),
            pltpu.VMEM((2 * zs, db, block), F32),
            pltpu.VMEM((poles, db, block), F32),
            dma,
            dma((chunks, devices)),
            dma((chunks, zs, 2)),
            dma((chunks, zs)),
            dma((chunks, 2, zs)),
            dma((chunks, poles)),
            dma((chunks, poles)),
            dma((2,)),
            dma((2,)),
            dma((2 * zs,)),
            dma((2 * zs,)),
            dma((poles,)),
            dma((poles,)),
        ],
        compiler_params=pltpu.CompilerParams(
            collective_id=0, has_side_effects=True, vmem_limit_bytes=60 * 1024 * 1024
        ),
    )(
        packed,
        inverse[0].reshape(2, devices, local_width, local_width),
        places,
        weight,
        own.reshape(1),
        dinv,
    )
    return panel.T, diag


def solution(mesh):
    placed = (
        P("pole", None, None, ("row", "col")),
        P("pole", None, ("row", "col"), None),
        P("pole", None, ("row", "col"), None),
        P(),
        P(),
        P(),
        P("pole"),
        P(),
    )
    return jax.shard_map(
        local,
        mesh=mesh,
        in_specs=placed,
        out_specs=(P(("row", "col"), None), P(("row", "col"), None)),
        check_vma=False,
    )
```

```python
import functools

import jax
import jax.numpy as jnp
from jax import lax
from jax.experimental import pallas as pl
from jax.experimental.pallas import tpu as pltpu
from jax.sharding import PartitionSpec as P

F32 = jnp.float32
BF16 = jnp.bfloat16
MESH = pl.DeviceIdType.MESH


def dot(left, right):
    return jnp.dot(left, right, preferred_element_type=F32)


def dot_nt(left, right):
    return lax.dot_general(left, right, (((1,), (1,)), ((), ())), preferred_element_type=F32)


def kernel(
    dims,
    factor_ref,
    inv_ref,
    dinv_ref,
    widths_ref,
    pattern_ref,
    owner_ref,
    assign_ref,
    weights_ref,
    panel_ref,
    diag_ref,
    factor,
    place_ref,
    pieces,
    inv,
    acc,
    shares,
    xe,
    le,
    gram,
    half,
    half_sum,
    parts,
    totals,
    factor_sem,
    inv_sem,
    recv,
    sz,
    sx,
    sc,
    ys,
    yr,
    d1s,
    d1r,
    d2s,
    d2r,
    d3s,
    d3r,
):
    chunks, zs, poles, width, blocks_k, block, db = dims
    pole = lax.axis_index("pole")
    row = lax.axis_index("row")
    z = lax.axis_index("col")
    hi = row // 2
    lo = row % 2
    sibling = hi * 2 + (1 - lo)
    across = (1 - hi) * 2 + lo

    def at(h, l, zz):
        return (h * 2 + l) * zs + zz

    me = at(hi, lo, z)
    mine = hi * zs + z

    barrier = pltpu.get_barrier_semaphore()
    pl.semaphore_signal(
        barrier, inc=1, device_id=(pole, sibling, z), device_id_type=MESH
    )

    @pl.loop(0, 2 * zs)
    def _(j):
        @pl.when(j != mine)
        def _():
            pl.semaphore_signal(
                barrier,
                inc=1,
                device_id=(pole, (j // zs) * 2 + lo, j % zs),
                device_id_type=MESH,
            )

    @pl.loop(0, poles)
    def _(p):
        @pl.when(p != pole)
        def _():
            pl.semaphore_signal(
                barrier, inc=1, device_id=(p, row, z), device_id_type=MESH
            )

    fetch = pltpu.make_async_copy(factor_ref, factor, factor_sem)
    fetch.start()
    load = pltpu.make_async_copy(inv_ref, inv, inv_sem)
    load.start()

    live = chunks * width
    local_width = factor.shape[1]
    starts = [jnp.int32(0)]
    for k in range(1, blocks_k):
        starts.append(starts[-1] + widths_ref[k - 1])
    slot = lax.broadcasted_iota(jnp.int32, (live, block), 0)
    position = lax.broadcasted_iota(jnp.int32, (live, block), 1)

    fetch.wait()
    for i in range(local_width // block):
        rows = slice(i * block, (i + 1) * block)
        found = [jnp.zeros((live, block), F32)] * 2
        for k in range(blocks_k):
            kept = widths_ref[k] * pattern_ref[me * (local_width // block) + i, k]
            hit = (slot == position + starts[k]) & (position < kept)
            pick = jnp.where(hit, 1.0, 0.0).astype(BF16)
            for part in range(2):
                found[part] += dot_nt(pick, factor[part, rows, k * block : (k + 1) * block])
        for part in range(2):
            packed = found[part].astype(BF16).reshape(chunks, width, block)
            pieces[:, me, part * width : (part + 1) * width, rows] = packed
    pl.semaphore_wait(barrier, 1 + (2 * zs - 1) + (poles - 1))

    def send(c, q, send_sem, to_row, to_col):
        return pltpu.make_async_remote_copy(
            src_ref=pieces.at[c, q],
            dst_ref=pieces.at[c, q],
            send_sem=send_sem,
            recv_sem=recv.at[c, q],
            device_id=(pole, to_row, to_col),
            device_id_type=MESH,
        )

    def up(c, h, zz):
        return send(c, at(h, lo, zz), sz.at[c, h, zz, 1], row, z + 1)

    def down(c, h, zz):
        return send(c, at(h, lo, zz), sz.at[c, h, zz, 0], row, z - 1)

    def cross(c, zz):
        return send(c, at(hi, lo, zz), sx.at[c, zz], across, z)

    def over(c, h, zz):
        return send(c, at(h, lo, zz), sc.at[c, h, zz], sibling, z)

    def arrived(c, q):
        send(c, q, sx.at[0, 0], across, z).wait_recv()

    def early(c, zz):
        return ((zz == 0) | (zz == zs - 1)) & (c % 2 == 1)

    def goes_up(zz):
        return (zz <= z) & (z < zs - 1)

    def goes_down(zz):
        return (zz >= z) & (z > 0)

    def crosses(c, zz):
        return (zz == z) | jnp.logical_not(early(c, zz))

    def forward(c, h, zz):
        @pl.when(goes_up(zz))
        def _():
            up(c, h, zz).start()

        @pl.when(goes_down(zz))
        def _():
            down(c, h, zz).start()

        over(c, h, zz).start()

    @pl.loop(0, chunks)
    def _(c):
        cross(c, z).start()
        forward(c, hi, z)

    source = lax.broadcasted_iota(jnp.int32, (block, width), 0)
    target = lax.broadcasted_iota(jnp.int32, (block, width), 1)

    @pl.loop(0, chunks)
    def _(c):
        for k in range(blocks_k):
            hit = (target + c * width == source + starts[k]) & (source < widths_ref[k])
            place_ref[c, k * block : (k + 1) * block] = jnp.where(hit, 1.0, 0.0).astype(BF16)

    acc[...] = jnp.zeros_like(acc)
    xe[...] = jnp.zeros_like(xe)
    le[...] = jnp.zeros_like(le)
    panel_ref[...] = jnp.zeros_like(panel_ref)
    load.wait()

    def compute(c, q):
        lt = pieces[c, q]
        u = dot(lt, inv[0, q])
        v = dot(lt, inv[1, q])
        acc[c, :width] += u[:width] - v[width:]
        acc[c, width:] += u[width:] + v[:width]

    def by_distance(visit, first):
        @pl.loop(first, 2 * zs)
        def _(j):
            s = j // 2
            zz = jnp.where(j % 2 == 0, z - s, z + s)

            @pl.when((zz >= 0) & (zz < zs) & (j != 1))
            def _():
                visit(zz)

    def along(c):
        def visit(zz):
            @pl.when(zz != z)
            def _():
                arrived(c, at(hi, lo, zz))

                @pl.when(crosses(c, zz))
                def _():
                    cross(c, zz).start()

                forward(c, hi, zz)

            compute(c, at(hi, lo, zz))

            @pl.when(early(c, zz))
            def _():
                arrived(c, at(1 - hi, lo, zz))
                forward(c, 1 - hi, zz)
                compute(c, at(1 - hi, lo, zz))

        by_distance(visit, 0)

    def crossed(c):
        def visit(zz):
            @pl.when(jnp.logical_not(early(c, zz)))
            def _():
                arrived(c, at(1 - hi, lo, zz))
                over(c, 1 - hi, zz).start()
                compute(c, at(1 - hi, lo, zz))

        by_distance(visit, 0)

    def from_sibling(c, h):
        def visit(zz):
            arrived(c, at(h, 1 - lo, zz))
            compute(c, at(h, 1 - lo, zz))

        by_distance(visit, 0)

    def share(c, p):
        return pltpu.make_async_remote_copy(
            src_ref=shares.at[c, pole],
            dst_ref=shares.at[c, pole],
            send_sem=ys.at[c, p],
            recv_sem=yr.at[c, pole],
            device_id=(p, row, z),
            device_id_type=MESH,
        )

    def share_from(c, p):
        return pltpu.make_async_remote_copy(
            src_ref=shares.at[c, p],
            dst_ref=shares.at[c, p],
            send_sem=ys.at[c, p],
            recv_sem=yr.at[c, p],
            device_id=(p, row, z),
            device_id_type=MESH,
        )

    wr = weights_ref[assign_ref[0], 0]
    wi = weights_ref[assign_ref[0], 1]

    def others(visit):
        @pl.loop(0, poles)
        def _(p):
            @pl.when(p != pole)
            def _():
                visit(p)

    def finish(c):
        xr = -acc[c, :width]
        xi = -acc[c, width:]
        shares[c, pole] = wr * xi + wi * xr
        others(lambda p: share(c, p).start())
        place = place_ref[c]
        xe[0] += dot(place, xr.astype(BF16)).astype(BF16)
        xe[1] += dot(place, xi.astype(BF16)).astype(BF16)

    def receive(c):
        others(lambda p: share_from(c, p).wait_recv())
        total = shares[c, 0]
        for p in range(1, poles):
            total = total + shares[c, p]
        total = total.T
        top = total.astype(BF16)
        rest = total - top.astype(F32)
        middle = rest.astype(BF16)
        low = (rest - middle.astype(F32)).astype(BF16)
        place = place_ref[c]
        terms = jnp.concatenate([top, middle, low], axis=1)
        panel_ref[...] += dot_nt(terms, jnp.concatenate([place] * 3, axis=1))

    @pl.loop(0, chunks + 2)
    def _(t):
        @pl.when(t >= 2)
        def _():
            from_sibling(t - 2, 1 - hi)
            finish(t - 2)

        @pl.when(t < chunks)
        def _():
            along(t)

        @pl.when((t >= 1) & (t <= chunks))
        def _():
            from_sibling(t - 1, hi)
            crossed(t - 1)

    @pl.loop(0, chunks)
    def _(c):
        lt = pieces[c, owner_ref[me]]
        place = place_ref[c]
        le[0] += dot(place, lt[:width]).astype(BF16)
        le[1] += dot(place, lt[width:]).astype(BF16)

    for k in range(blocks_k):
        rows = slice(k * block, (k + 1) * block)
        lr, li, xr, xi = le[0, rows], le[1, rows], xe[0, rows], xe[1, rows]
        real = dot_nt(lr, xr) - dot_nt(li, xi)
        imag = dot_nt(lr, xi) + dot_nt(li, xr)
        gram[rows] = wr * imag + wi * real

    span = zs * db

    def rows_of(h, l):
        return pl.ds(pl.multiple_of((h * 2 + l) * span, 8), span)

    halves = []
    for h in range(2):
        halves.append(
            pltpu.make_async_remote_copy(
                src_ref=gram.at[rows_of(h, 1 - lo)],
                dst_ref=half.at[h],
                send_sem=d1s.at[h],
                recv_sem=d1r.at[h],
                device_id=(pole, sibling, z),
                device_id_type=MESH,
            )
        )
        halves[h].start()

    @pl.loop(0, chunks - 1)
    def _(c):
        receive(c)

    for h in range(2):
        halves[h].wait_recv()
        half_sum[h] = (gram[rows_of(h, lo)] + half[h]).reshape(zs, db, block)

    def part(j):
        return pltpu.make_async_remote_copy(
            src_ref=half_sum.at[j // zs, j % zs],
            dst_ref=parts.at[mine],
            send_sem=d2s.at[j],
            recv_sem=d2r.at[mine],
            device_id=(pole, (j // zs) * 2 + lo, j % zs),
            device_id_type=MESH,
        )

    def part_from(j):
        return pltpu.make_async_remote_copy(
            src_ref=parts.at[j],
            dst_ref=parts.at[j],
            send_sem=d2s.at[j],
            recv_sem=d2r.at[j],
            device_id=(pole, (j // zs) * 2 + lo, j % zs),
            device_id_type=MESH,
        )

    def peers(visit):
        @pl.loop(0, 2 * zs)
        def _(j):
            @pl.when(j != mine)
            def _():
                visit(j)

    peers(lambda j: part(j).start())
    parts[mine] = half_sum[hi, z]
    receive(chunks - 1)
    peers(lambda j: part_from(j).wait_recv())
    total = parts[0]
    for j in range(1, 2 * zs):
        total = total + parts[j]
    dinv = dinv_ref[...].astype(F32)
    totals[pole] = (wr * dinv[1] + wi * dinv[0]) - total

    def result(p, slot):
        return pltpu.make_async_remote_copy(
            src_ref=totals.at[slot],
            dst_ref=totals.at[slot],
            send_sem=d3s.at[p],
            recv_sem=d3r.at[slot],
            device_id=(p, row, z),
            device_id_type=MESH,
        )

    others(lambda p: result(p, pole).start())

    @pl.loop(0, chunks)
    def _(c):
        @pl.loop(0, zs)
        def _(zz):
            over(c, 0, zz).wait_send()
            over(c, 1, zz).wait_send()

            @pl.when(crosses(c, zz))
            def _():
                cross(c, zz).wait_send()

            for h in range(2):
                travels = (h == hi) | early(c, zz)

                @pl.when(travels & goes_up(zz))
                def _():
                    up(c, h, zz).wait_send()

                @pl.when(travels & goes_down(zz))
                def _():
                    down(c, h, zz).wait_send()

        others(lambda p: share(c, p).wait_send())

    for h in range(2):
        halves[h].wait_send()
    peers(lambda j: part(j).wait_send())
    others(lambda p: result(p, p).wait_recv())
    final = totals[0]
    for p in range(1, poles):
        final = final + totals[p]
    diag_ref[...] = final
    others(lambda p: result(p, pole).wait_send())


def local(inverse, factor, diag_inverse, widths, pattern, owner, assign, pole_weights):
    zs = lax.axis_size("col")
    poles = lax.axis_size("pole")
    rows_n = lax.axis_size("row")
    assert rows_n == 4
    devices = rows_n * zs
    local_width = factor.shape[2]
    total_cols = factor.shape[3]
    db = diag_inverse.shape[2]
    block = diag_inverse.shape[3]
    blocks_k = total_cols // block
    live = 2 * total_cols // 3
    width = 128
    chunks = live // width

    dims = (chunks, zs, poles, width, blocks_k, block, db)
    vmem = pl.BlockSpec(memory_space=pltpu.VMEM)
    hbm = pl.BlockSpec(memory_space=pl.ANY)
    smem = pl.BlockSpec(memory_space=pltpu.SMEM)
    dma = pltpu.SemaphoreType.DMA
    return pl.pallas_call(
        functools.partial(kernel, dims),
        out_shape=(
            jax.ShapeDtypeStruct((local_width, total_cols), F32),
            jax.ShapeDtypeStruct((db, block), F32),
        ),
        in_specs=[hbm, hbm, vmem, smem, smem, smem, smem, smem],
        out_specs=(vmem, vmem),
        scratch_shapes=[
            pltpu.VMEM((2, local_width, total_cols), BF16),
            pltpu.VMEM((chunks, total_cols, width), BF16),
            pltpu.VMEM((chunks, devices, 2 * width, local_width), BF16),
            pltpu.VMEM((2, devices, local_width, local_width), BF16),
            pltpu.VMEM((chunks, 2 * width, local_width), F32),
            pltpu.VMEM((chunks, poles, width, local_width), F32),
            pltpu.VMEM((2, total_cols, local_width), BF16),
            pltpu.VMEM((2, total_cols, local_width), BF16),
            pltpu.VMEM((total_cols, block), F32),
            pltpu.VMEM((2, zs * db, block), F32),
            pltpu.VMEM((2, zs, db, block), F32),
            pltpu.VMEM((2 * zs, db, block), F32),
            pltpu.VMEM((poles, db, block), F32),
            dma,
            dma,
            dma((chunks, devices)),
            dma((chunks, 2, zs, 2)),
            dma((chunks, zs)),
            dma((chunks, 2, zs)),
            dma((chunks, poles)),
            dma((chunks, poles)),
            dma((2,)),
            dma((2,)),
            dma((2 * zs,)),
            dma((2 * zs,)),
            dma((poles,)),
            dma((poles,)),
        ],
        compiler_params=pltpu.CompilerParams(
            collective_id=0, has_side_effects=True, vmem_limit_bytes=60 * 1024 * 1024
        ),
    )(
        factor[0],
        inverse[0].reshape(2, devices, local_width, local_width),
        diag_inverse[0],
        widths,
        pattern,
        owner,
        assign,
        pole_weights,
    )


def solution(mesh):
    placed = (
        P("pole", None, None, ("row", "col")),
        P("pole", None, ("row", "col"), None),
        P("pole", None, ("row", "col"), None),
        P(),
        P(),
        P(),
        P("pole"),
        P(),
    )
    return jax.shard_map(
        local,
        mesh=mesh,
        in_specs=placed,
        out_specs=(P(("row", "col"), None), P(("row", "col"), None)),
        check_vma=False,
    )
```

```python
import functools

import jax
import jax.numpy as jnp
from jax import lax
from jax.experimental import pallas as pl
from jax.experimental.pallas import tpu as pltpu
from jax.sharding import PartitionSpec as P

F32 = jnp.float32
BF16 = jnp.bfloat16
MESH = pl.DeviceIdType.MESH


def dot(left, right):
    return jnp.dot(left, right, preferred_element_type=F32)


def dot_nt(left, right):
    return lax.dot_general(left, right, (((1,), (1,)), ((), ())), preferred_element_type=F32)


def kernel(
    dims,
    factor_ref,
    inv_ref,
    dinv_ref,
    widths_ref,
    pattern_ref,
    owner_ref,
    assign_ref,
    weights_ref,
    panel_ref,
    diag_ref,
    factor,
    place_ref,
    pieces,
    inv,
    acc,
    shares,
    xe,
    le,
    gram,
    half,
    half_sum,
    parts,
    totals,
    factor_sem,
    inv_sem,
    recv,
    sz,
    sx,
    sc,
    ys,
    yr,
    d1s,
    d1r,
    d2s,
    d2r,
    d3s,
    d3r,
):
    chunks, zs, poles, width, blocks_k, block, db = dims
    pole = lax.axis_index("pole")
    row = lax.axis_index("row")
    z = lax.axis_index("col")
    hi = row // 2
    lo = row % 2
    sibling = hi * 2 + (1 - lo)
    across = (1 - hi) * 2 + lo

    def at(h, l, zz):
        return (h * 2 + l) * zs + zz

    me = at(hi, lo, z)
    mine = hi * zs + z

    barrier = pltpu.get_barrier_semaphore()
    pl.semaphore_signal(
        barrier, inc=1, device_id=(pole, sibling, z), device_id_type=MESH
    )

    @pl.loop(0, 2 * zs)
    def _(j):
        @pl.when(j != mine)
        def _():
            pl.semaphore_signal(
                barrier,
                inc=1,
                device_id=(pole, (j // zs) * 2 + lo, j % zs),
                device_id_type=MESH,
            )

    @pl.loop(0, poles)
    def _(p):
        @pl.when(p != pole)
        def _():
            pl.semaphore_signal(
                barrier, inc=1, device_id=(p, row, z), device_id_type=MESH
            )

    fetch = pltpu.make_async_copy(factor_ref, factor, factor_sem)
    fetch.start()
    load = pltpu.make_async_copy(inv_ref, inv, inv_sem)
    load.start()

    live = chunks * width
    local_width = factor.shape[1]
    starts = [jnp.int32(0)]
    for k in range(1, blocks_k):
        starts.append(starts[-1] + widths_ref[k - 1])
    slot = lax.broadcasted_iota(jnp.int32, (live, block), 0)
    position = lax.broadcasted_iota(jnp.int32, (live, block), 1)

    fetch.wait()
    for i in range(local_width // block):
        rows = slice(i * block, (i + 1) * block)
        found = [jnp.zeros((live, block), F32)] * 2
        kinds = pattern_ref[pl.ds(me * (local_width // block) + i, 1), :]
        for k in range(blocks_k):
            kept = widths_ref[k] * kinds[:, k : k + 1]
            hit = (slot == position + starts[k]) & (position < kept)
            pick = jnp.where(hit, 1.0, 0.0).astype(BF16)
            for part in range(2):
                found[part] += dot_nt(pick, factor[part, rows, k * block : (k + 1) * block])
        for part in range(2):
            packed = found[part].astype(BF16).reshape(chunks, width, block)
            pieces[:, me, part * width : (part + 1) * width, rows] = packed
    pl.semaphore_wait(barrier, 1 + (2 * zs - 1) + (poles - 1))

    def send(c, q, send_sem, to_row, to_col):
        return pltpu.make_async_remote_copy(
            src_ref=pieces.at[c, q],
            dst_ref=pieces.at[c, q],
            send_sem=send_sem,
            recv_sem=recv.at[c, q],
            device_id=(pole, to_row, to_col),
            device_id_type=MESH,
        )

    def up(c, h, zz):
        return send(c, at(h, lo, zz), sz.at[c, h, zz, 1], row, z + 1)

    def down(c, h, zz):
        return send(c, at(h, lo, zz), sz.at[c, h, zz, 0], row, z - 1)

    def cross(c, zz):
        return send(c, at(hi, lo, zz), sx.at[c, zz], across, z)

    def over(c, h, zz):
        return send(c, at(h, lo, zz), sc.at[c, h, zz], sibling, z)

    def arrived(c, q):
        send(c, q, sx.at[0, 0], across, z).wait_recv()

    def goes_up(zz):
        return (zz <= z) & (z < zs - 1)

    def goes_down(zz):
        return (zz >= z) & (z > 0)

    def forward(c, h, zz):
        @pl.when(goes_up(zz))
        def _():
            up(c, h, zz).start()

        @pl.when(goes_down(zz))
        def _():
            down(c, h, zz).start()

        over(c, h, zz).start()

    def begin(c):
        cross(c, z).start()
        forward(c, hi, z)

    for c in range(min(2, chunks)):
        begin(c)

    source = lax.broadcasted_iota(jnp.int32, (block, width), 0)
    target = lax.broadcasted_iota(jnp.int32, (block, width), 1)

    @pl.loop(0, chunks)
    def _(c):
        for k in range(blocks_k):
            hit = (target + c * width == source + starts[k]) & (source < widths_ref[k])
            place_ref[c, k * block : (k + 1) * block] = jnp.where(hit, 1.0, 0.0).astype(BF16)

    acc[...] = jnp.zeros_like(acc)
    xe[...] = jnp.zeros_like(xe)
    le[...] = jnp.zeros_like(le)
    panel_ref[...] = jnp.zeros_like(panel_ref)
    load.wait()

    def compute(c, q):
        lt = pieces[c, q]
        u = dot(lt, inv[0, q])
        v = dot(lt, inv[1, q])
        acc[c, :width] += u[:width] - v[width:]
        acc[c, width:] += u[width:] + v[:width]

    def share(c, p):
        return pltpu.make_async_remote_copy(
            src_ref=shares.at[c, pole],
            dst_ref=shares.at[c, pole],
            send_sem=ys.at[c, p],
            recv_sem=yr.at[c, pole],
            device_id=(p, row, z),
            device_id_type=MESH,
        )

    def share_from(c, p):
        return pltpu.make_async_remote_copy(
            src_ref=shares.at[c, p],
            dst_ref=shares.at[c, p],
            send_sem=ys.at[c, p],
            recv_sem=yr.at[c, p],
            device_id=(p, row, z),
            device_id_type=MESH,
        )

    chosen = lax.broadcasted_iota(jnp.int32, weights_ref.shape, 0) == assign_ref[0]
    weight = jnp.sum(jnp.where(chosen, weights_ref[...], 0.0), axis=0, keepdims=True)
    wr = weight[:, 0:1]
    wi = weight[:, 1:2]

    def others(visit):
        @pl.loop(0, poles)
        def _(p):
            @pl.when(p != pole)
            def _():
                visit(p)

    def finish(c):
        xr = -acc[c, :width]
        xi = -acc[c, width:]
        shares[c, pole] = wr * xi + wi * xr
        others(lambda p: share(c, p).start())
        place = place_ref[c]
        xe[0] += dot(place, xr.astype(BF16)).astype(BF16)
        xe[1] += dot(place, xi.astype(BF16)).astype(BF16)

    def receive(c):
        others(lambda p: share_from(c, p).wait_recv())
        total = shares[c, 0]
        for p in range(1, poles):
            total = total + shares[c, p]
        total = total.T
        top = total.astype(BF16)
        rest = total - top.astype(F32)
        middle = rest.astype(BF16)
        low = (rest - middle.astype(F32)).astype(BF16)
        place = place_ref[c]
        terms = jnp.concatenate([top, middle, low], axis=1)
        panel_ref[...] += dot_nt(terms, jnp.concatenate([place] * 3, axis=1))

    @pl.loop(0, chunks + 2)
    def _(t):
        @pl.when(t < chunks - 2)
        def _():
            begin(t + 2)

        @pl.loop(0, 2 * zs)
        def _(j):
            s = j // 2
            zz = jnp.where(j % 2 == 0, z - s, z + s)

            @pl.when((zz >= 0) & (zz < zs) & (j != 1))
            def _():
                @pl.when((t < chunks) & (zz != z))
                def _():
                    arrived(t, at(hi, lo, zz))
                    cross(t, zz).start()
                    forward(t, hi, zz)

                @pl.when((t >= 1) & (t <= chunks))
                def _():
                    arrived(t - 1, at(1 - hi, lo, zz))
                    over(t - 1, 1 - hi, zz).start()
                    compute(t - 1, at(hi, lo, zz))
                    arrived(t - 1, at(hi, 1 - lo, zz))
                    compute(t - 1, at(hi, 1 - lo, zz))
                    compute(t - 1, at(1 - hi, lo, zz))

                @pl.when(t >= 2)
                def _():
                    arrived(t - 2, at(1 - hi, 1 - lo, zz))
                    compute(t - 2, at(1 - hi, 1 - lo, zz))

        @pl.when(t >= 2)
        def _():
            finish(t - 2)

    @pl.loop(0, chunks)
    def _(c):
        lt = pieces[c, owner_ref[me]]
        place = place_ref[c]
        le[0] += dot(place, lt[:width]).astype(BF16)
        le[1] += dot(place, lt[width:]).astype(BF16)

    for k in range(blocks_k):
        rows = slice(k * block, (k + 1) * block)
        lr, li, xr, xi = le[0, rows], le[1, rows], xe[0, rows], xe[1, rows]
        real = dot_nt(lr, xr) - dot_nt(li, xi)
        imag = dot_nt(lr, xi) + dot_nt(li, xr)
        gram[rows] = wr * imag + wi * real

    span = zs * db

    def rows_of(h, l):
        return pl.ds(pl.multiple_of((h * 2 + l) * span, 8), span)

    halves = []
    for h in range(2):
        halves.append(
            pltpu.make_async_remote_copy(
                src_ref=gram.at[rows_of(h, 1 - lo)],
                dst_ref=half.at[h],
                send_sem=d1s.at[h],
                recv_sem=d1r.at[h],
                device_id=(pole, sibling, z),
                device_id_type=MESH,
            )
        )
        halves[h].start()

    @pl.loop(0, chunks - 1)
    def _(c):
        receive(c)

    for h in range(2):
        halves[h].wait_recv()
        half_sum[h] = (gram[rows_of(h, lo)] + half[h]).reshape(zs, db, block)

    def part(j):
        return pltpu.make_async_remote_copy(
            src_ref=half_sum.at[j // zs, j % zs],
            dst_ref=parts.at[mine],
            send_sem=d2s.at[j],
            recv_sem=d2r.at[mine],
            device_id=(pole, (j // zs) * 2 + lo, j % zs),
            device_id_type=MESH,
        )

    def part_from(j):
        return pltpu.make_async_remote_copy(
            src_ref=parts.at[j],
            dst_ref=parts.at[j],
            send_sem=d2s.at[j],
            recv_sem=d2r.at[j],
            device_id=(pole, (j // zs) * 2 + lo, j % zs),
            device_id_type=MESH,
        )

    def peers(visit):
        @pl.loop(0, 2 * zs)
        def _(j):
            @pl.when(j != mine)
            def _():
                visit(j)

    peers(lambda j: part(j).start())
    parts[mine] = half_sum[hi, z]
    receive(chunks - 1)
    peers(lambda j: part_from(j).wait_recv())
    total = parts[0]
    for j in range(1, 2 * zs):
        total = total + parts[j]
    dinv = dinv_ref[...].astype(F32)
    totals[pole] = (wr * dinv[1] + wi * dinv[0]) - total

    def result(p, slot):
        return pltpu.make_async_remote_copy(
            src_ref=totals.at[slot],
            dst_ref=totals.at[slot],
            send_sem=d3s.at[p],
            recv_sem=d3r.at[slot],
            device_id=(p, row, z),
            device_id_type=MESH,
        )

    others(lambda p: result(p, pole).start())

    @pl.loop(0, chunks)
    def _(c):
        @pl.loop(0, zs)
        def _(zz):
            over(c, 0, zz).wait_send()
            over(c, 1, zz).wait_send()

            cross(c, zz).wait_send()

            @pl.when(goes_up(zz))
            def _():
                up(c, hi, zz).wait_send()

            @pl.when(goes_down(zz))
            def _():
                down(c, hi, zz).wait_send()

        others(lambda p: share(c, p).wait_send())

    for h in range(2):
        halves[h].wait_send()
    peers(lambda j: part(j).wait_send())
    others(lambda p: result(p, p).wait_recv())
    final = totals[0]
    for p in range(1, poles):
        final = final + totals[p]
    diag_ref[...] = final
    others(lambda p: result(p, pole).wait_send())


def local(inverse, factor, diag_inverse, widths, pattern, owner, assign, pole_weights):
    zs = lax.axis_size("col")
    poles = lax.axis_size("pole")
    rows_n = lax.axis_size("row")
    assert rows_n == 4
    devices = rows_n * zs
    local_width = factor.shape[2]
    total_cols = factor.shape[3]
    db = diag_inverse.shape[2]
    block = diag_inverse.shape[3]
    blocks_k = total_cols // block
    live = 2 * total_cols // 3
    width = 128
    chunks = live // width

    dims = (chunks, zs, poles, width, blocks_k, block, db)
    vmem = pl.BlockSpec(memory_space=pltpu.VMEM)
    hbm = pl.BlockSpec(memory_space=pl.ANY)
    smem = pl.BlockSpec(memory_space=pltpu.SMEM)
    dma = pltpu.SemaphoreType.DMA
    return pl.pallas_call(
        functools.partial(kernel, dims),
        out_shape=(
            jax.ShapeDtypeStruct((local_width, total_cols), F32),
            jax.ShapeDtypeStruct((db, block), F32),
        ),
        in_specs=[hbm, hbm, vmem, smem, vmem, smem, smem, vmem],
        out_specs=(vmem, vmem),
        scratch_shapes=[
            pltpu.VMEM((2, local_width, total_cols), BF16),
            pltpu.VMEM((chunks, total_cols, width), BF16),
            pltpu.VMEM((chunks, devices, 2 * width, local_width), BF16),
            pltpu.VMEM((2, devices, local_width, local_width), BF16),
            pltpu.VMEM((chunks, 2 * width, local_width), F32),
            pltpu.VMEM((chunks, poles, width, local_width), F32),
            pltpu.VMEM((2, total_cols, local_width), BF16),
            pltpu.VMEM((2, total_cols, local_width), BF16),
            pltpu.VMEM((total_cols, block), F32),
            pltpu.VMEM((2, zs * db, block), F32),
            pltpu.VMEM((2, zs, db, block), F32),
            pltpu.VMEM((2 * zs, db, block), F32),
            pltpu.VMEM((poles, db, block), F32),
            dma,
            dma,
            dma((chunks, devices)),
            dma((chunks, 2, zs, 2)),
            dma((chunks, zs)),
            dma((chunks, 2, zs)),
            dma((chunks, poles)),
            dma((chunks, poles)),
            dma((2,)),
            dma((2,)),
            dma((2 * zs,)),
            dma((2 * zs,)),
            dma((poles,)),
            dma((poles,)),
        ],
        compiler_params=pltpu.CompilerParams(
            collective_id=0, has_side_effects=True, vmem_limit_bytes=60 * 1024 * 1024
        ),
    )(
        factor[0],
        inverse[0].reshape(2, devices, local_width, local_width),
        diag_inverse[0],
        widths,
        pattern,
        owner,
        assign,
        pole_weights,
    )


def solution(mesh):
    placed = (
        P("pole", None, None, ("row", "col")),
        P("pole", None, ("row", "col"), None),
        P("pole", None, ("row", "col"), None),
        P(),
        P(),
        P(),
        P("pole"),
        P(),
    )
    return jax.shard_map(
        local,
        mesh=mesh,
        in_specs=placed,
        out_specs=(P(("row", "col"), None), P(("row", "col"), None)),
        check_vma=False,
    )
```

```python
import functools

import jax
import jax.numpy as jnp
from jax import lax
from jax.experimental import pallas as pl
from jax.experimental.pallas import tpu as pltpu
from jax.sharding import PartitionSpec as P

F32 = jnp.float32
BF16 = jnp.bfloat16
MESH = pl.DeviceIdType.MESH


def dot(left, right):
    return jnp.dot(left, right, preferred_element_type=F32)


def dot_nt(left, right):
    return lax.dot_general(left, right, (((1,), (1,)), ((), ())), preferred_element_type=F32)


def kernel(
    dims,
    factor_ref,
    inv_ref,
    dinv_ref,
    widths_ref,
    pattern_ref,
    owner_ref,
    assign_ref,
    weights_ref,
    panel_ref,
    diag_ref,
    factor,
    place_ref,
    pieces,
    inv,
    acc,
    shares,
    xe,
    le,
    gram,
    half,
    half_sum,
    parts,
    totals,
    factor_sem,
    inv_sem,
    recv,
    sz,
    sd,
    sx,
    sc,
    ys,
    yr,
    d1s,
    d1r,
    d2s,
    d2r,
    d3s,
    d3r,
):
    chunks, zs, poles, width, blocks_k, block, db = dims
    pole = lax.axis_index("pole")
    row = lax.axis_index("row")
    z = lax.axis_index("col")
    hi = row // 2
    lo = row % 2
    sibling = hi * 2 + (1 - lo)
    across = (1 - hi) * 2 + lo

    def at(h, l, zz):
        return (h * 2 + l) * zs + zz

    me = at(hi, lo, z)
    mine = hi * zs + z

    barrier = pltpu.get_barrier_semaphore()
    pl.semaphore_signal(
        barrier, inc=1, device_id=(pole, sibling, z), device_id_type=MESH
    )

    @pl.loop(0, 2 * zs)
    def _(j):
        @pl.when(j != mine)
        def _():
            pl.semaphore_signal(
                barrier,
                inc=1,
                device_id=(pole, (j // zs) * 2 + lo, j % zs),
                device_id_type=MESH,
            )

    @pl.loop(0, poles)
    def _(p):
        @pl.when(p != pole)
        def _():
            pl.semaphore_signal(
                barrier, inc=1, device_id=(p, row, z), device_id_type=MESH
            )

    fetch = pltpu.make_async_copy(factor_ref, factor, factor_sem)
    fetch.start()
    load = pltpu.make_async_copy(inv_ref, inv, inv_sem)
    load.start()

    live = chunks * width
    local_width = factor.shape[1]
    starts = [jnp.int32(0)]
    for k in range(1, blocks_k):
        starts.append(starts[-1] + widths_ref[k - 1])
    slot = lax.broadcasted_iota(jnp.int32, (live, block), 0)
    position = lax.broadcasted_iota(jnp.int32, (live, block), 1)

    fetch.wait()
    for i in range(local_width // block):
        rows = slice(i * block, (i + 1) * block)
        found = [jnp.zeros((live, block), F32)] * 2
        here = lax.broadcasted_iota(jnp.int32, pattern_ref.shape, 1)
        here = here == me * (local_width // block) + i
        kinds = jnp.sum(jnp.where(here, pattern_ref[...], 0), axis=1, keepdims=True)
        for k in range(blocks_k):
            kept = widths_ref[k] * kinds[k : k + 1]
            hit = (slot == position + starts[k]) & (position < kept)
            pick = jnp.where(hit, 1.0, 0.0).astype(BF16)
            for part in range(2):
                found[part] += dot_nt(pick, factor[part, rows, k * block : (k + 1) * block])
        for part in range(2):
            packed = found[part].astype(BF16).reshape(chunks, width, block)
            pieces[:, me, part * width : (part + 1) * width, rows] = packed
    pl.semaphore_wait(barrier, 1 + (2 * zs - 1) + (poles - 1))

    def send(c, q, send_sem, to_row, to_col):
        return pltpu.make_async_remote_copy(
            src_ref=pieces.at[c, q],
            dst_ref=pieces.at[c, q],
            send_sem=send_sem,
            recv_sem=recv.at[c, q],
            device_id=(pole, to_row, to_col),
            device_id_type=MESH,
        )

    def up(c, zz):
        return send(c, at(hi, lo, zz), sz.at[c, zz, 1], row, z + 1)

    def down(c, zz):
        return send(c, at(hi, lo, zz), sz.at[c, zz, 0], row, z - 1)

    def straight(c, zz):
        return send(c, me, sd.at[c, zz], row, zz)

    def cross(c, zz):
        return send(c, at(hi, lo, zz), sx.at[c, zz], across, z)

    def over(c, h, zz):
        return send(c, at(h, lo, zz), sc.at[c, h, zz], sibling, z)

    def arrived(c, q):
        send(c, q, sx.at[0, 0], across, z).wait_recv()

    def inner(zz):
        return (zz > 0) & (zz < zs - 1)

    def goes_up(zz):
        return inner(zz) & (zz <= z) & (z < zs - 1)

    def goes_down(zz):
        return inner(zz) & (zz >= z) & (z > 0)

    def along(visit_up, visit_down, zz):
        @pl.when(goes_up(zz))
        def _():
            visit_up()

        @pl.when(goes_down(zz))
        def _():
            visit_down()

    def from_end(visit):
        @pl.when(jnp.logical_not(inner(z)))
        def _():
            @pl.loop(1, zs)
            def _(s):
                visit(jnp.where(z == 0, s, zs - 1 - s))

    def forward(c, zz):
        along(lambda: up(c, zz).start(), lambda: down(c, zz).start(), zz)
        cross(c, zz).start()
        over(c, hi, zz).start()

    @pl.loop(0, chunks)
    def _(c):
        from_end(lambda zz: straight(c, zz).start())
        forward(c, z)

    source = lax.broadcasted_iota(jnp.int32, (block, width), 0)
    target = lax.broadcasted_iota(jnp.int32, (block, width), 1)

    @pl.loop(0, chunks)
    def _(c):
        for k in range(blocks_k):
            hit = (target + c * width == source + starts[k]) & (source < widths_ref[k])
            place_ref[c, k * block : (k + 1) * block] = jnp.where(hit, 1.0, 0.0).astype(BF16)

    acc[...] = jnp.zeros_like(acc)
    xe[...] = jnp.zeros_like(xe)
    le[...] = jnp.zeros_like(le)
    panel_ref[...] = jnp.zeros_like(panel_ref)
    load.wait()

    def compute(c, q):
        lt = pieces[c, q]
        u = dot(lt, inv[0, q])
        v = dot(lt, inv[1, q])
        acc[c, :width] += u[:width] - v[width:]
        acc[c, width:] += u[width:] + v[:width]

    def share(c, p):
        return pltpu.make_async_remote_copy(
            src_ref=shares.at[c, pole],
            dst_ref=shares.at[c, pole],
            send_sem=ys.at[c, p],
            recv_sem=yr.at[c, pole],
            device_id=(p, row, z),
            device_id_type=MESH,
        )

    def share_from(c, p):
        return pltpu.make_async_remote_copy(
            src_ref=shares.at[c, p],
            dst_ref=shares.at[c, p],
            send_sem=ys.at[c, p],
            recv_sem=yr.at[c, p],
            device_id=(p, row, z),
            device_id_type=MESH,
        )

    chosen = lax.broadcasted_iota(jnp.int32, weights_ref.shape, 1) == assign_ref[0]
    weight = jnp.sum(jnp.where(chosen, weights_ref[...], 0.0), axis=1, keepdims=True)
    wr = weight[0:1]
    wi = weight[1:2]

    def others(visit):
        @pl.loop(0, poles)
        def _(p):
            @pl.when(p != pole)
            def _():
                visit(p)

    def finish(c):
        xr = -acc[c, :width]
        xi = -acc[c, width:]
        shares[c, pole] = wr * xi + wi * xr
        others(lambda p: share(c, p).start())
        place = place_ref[c]
        xe[0] += dot(place, xr.astype(BF16)).astype(BF16)
        xe[1] += dot(place, xi.astype(BF16)).astype(BF16)

    def receive(c):
        others(lambda p: share_from(c, p).wait_recv())
        total = shares[c, 0]
        for p in range(1, poles):
            total = total + shares[c, p]
        total = total.T
        top = total.astype(BF16)
        rest = total - top.astype(F32)
        middle = rest.astype(BF16)
        low = (rest - middle.astype(F32)).astype(BF16)
        place = place_ref[c]
        terms = jnp.concatenate([top, middle, low], axis=1)
        panel_ref[...] += dot_nt(terms, jnp.concatenate([place] * 3, axis=1))

    @pl.loop(0, chunks + 2)
    def _(t):
        @pl.loop(0, 2 * zs)
        def _(j):
            s = j // 2
            zz = jnp.where(j % 2 == 0, z - s, z + s)

            @pl.when((zz >= 0) & (zz < zs) & (j != 1))
            def _():
                @pl.when(t < chunks)
                def _():
                    @pl.when(zz != z)
                    def _():
                        arrived(t, at(hi, lo, zz))
                        forward(t, zz)

                    compute(t, at(hi, lo, zz))

                @pl.when((t >= 1) & (t <= chunks))
                def _():
                    arrived(t - 1, at(1 - hi, lo, zz))
                    over(t - 1, 1 - hi, zz).start()
                    arrived(t - 1, at(hi, 1 - lo, zz))
                    compute(t - 1, at(hi, 1 - lo, zz))
                    compute(t - 1, at(1 - hi, lo, zz))

                @pl.when(t >= 2)
                def _():
                    arrived(t - 2, at(1 - hi, 1 - lo, zz))
                    compute(t - 2, at(1 - hi, 1 - lo, zz))

        @pl.when(t >= 2)
        def _():
            finish(t - 2)

    @pl.loop(0, chunks)
    def _(c):
        lt = pieces[c, owner_ref[me]]
        place = place_ref[c]
        le[0] += dot(place, lt[:width]).astype(BF16)
        le[1] += dot(place, lt[width:]).astype(BF16)

    for k in range(blocks_k):
        rows = slice(k * block, (k + 1) * block)
        lr, li, xr, xi = le[0, rows], le[1, rows], xe[0, rows], xe[1, rows]
        real = dot_nt(lr, xr) - dot_nt(li, xi)
        imag = dot_nt(lr, xi) + dot_nt(li, xr)
        gram[rows] = wr * imag + wi * real

    span = zs * db

    def rows_of(h, l):
        return pl.ds(pl.multiple_of((h * 2 + l) * span, 8), span)

    halves = []
    for h in range(2):
        halves.append(
            pltpu.make_async_remote_copy(
                src_ref=gram.at[rows_of(h, 1 - lo)],
                dst_ref=half.at[h],
                send_sem=d1s.at[h],
                recv_sem=d1r.at[h],
                device_id=(pole, sibling, z),
                device_id_type=MESH,
            )
        )
        halves[h].start()

    @pl.loop(0, chunks - 1)
    def _(c):
        receive(c)

    for h in range(2):
        halves[h].wait_recv()
        half_sum[h] = (gram[rows_of(h, lo)] + half[h]).reshape(zs, db, block)

    def part(j):
        return pltpu.make_async_remote_copy(
            src_ref=half_sum.at[j // zs, j % zs],
            dst_ref=parts.at[mine],
            send_sem=d2s.at[j],
            recv_sem=d2r.at[mine],
            device_id=(pole, (j // zs) * 2 + lo, j % zs),
            device_id_type=MESH,
        )

    def part_from(j):
        return pltpu.make_async_remote_copy(
            src_ref=parts.at[j],
            dst_ref=parts.at[j],
            send_sem=d2s.at[j],
            recv_sem=d2r.at[j],
            device_id=(pole, (j // zs) * 2 + lo, j % zs),
            device_id_type=MESH,
        )

    def peers(visit):
        @pl.loop(0, 2 * zs)
        def _(j):
            @pl.when(j != mine)
            def _():
                visit(j)

    peers(lambda j: part(j).start())
    parts[mine] = half_sum[hi, z]
    receive(chunks - 1)
    peers(lambda j: part_from(j).wait_recv())
    total = parts[0]
    for j in range(1, 2 * zs):
        total = total + parts[j]
    dinv = dinv_ref[...].astype(F32)
    totals[pole] = (wr * dinv[1] + wi * dinv[0]) - total

    def result(p, slot):
        return pltpu.make_async_remote_copy(
            src_ref=totals.at[slot],
            dst_ref=totals.at[slot],
            send_sem=d3s.at[p],
            recv_sem=d3r.at[slot],
            device_id=(p, row, z),
            device_id_type=MESH,
        )

    others(lambda p: result(p, pole).start())

    @pl.loop(0, chunks)
    def _(c):
        @pl.loop(0, zs)
        def _(zz):
            over(c, 0, zz).wait_send()
            over(c, 1, zz).wait_send()

            cross(c, zz).wait_send()

            along(lambda: up(c, zz).wait_send(), lambda: down(c, zz).wait_send(), zz)

        from_end(lambda zz: straight(c, zz).wait_send())
        others(lambda p: share(c, p).wait_send())

    for h in range(2):
        halves[h].wait_send()
    peers(lambda j: part(j).wait_send())
    others(lambda p: result(p, p).wait_recv())
    final = totals[0]
    for p in range(1, poles):
        final = final + totals[p]
    diag_ref[...] = final
    others(lambda p: result(p, pole).wait_send())


def local(inverse, factor, diag_inverse, widths, pattern, owner, assign, pole_weights):
    zs = lax.axis_size("col")
    poles = lax.axis_size("pole")
    rows_n = lax.axis_size("row")
    assert rows_n == 4
    devices = rows_n * zs
    local_width = factor.shape[2]
    total_cols = factor.shape[3]
    db = diag_inverse.shape[2]
    block = diag_inverse.shape[3]
    blocks_k = total_cols // block
    live = 2 * total_cols // 3
    width = 128
    chunks = live // width

    dims = (chunks, zs, poles, width, blocks_k, block, db)
    vmem = pl.BlockSpec(memory_space=pltpu.VMEM)
    hbm = pl.BlockSpec(memory_space=pl.ANY)
    smem = pl.BlockSpec(memory_space=pltpu.SMEM)
    dma = pltpu.SemaphoreType.DMA
    return pl.pallas_call(
        functools.partial(kernel, dims),
        out_shape=(
            jax.ShapeDtypeStruct((local_width, total_cols), F32),
            jax.ShapeDtypeStruct((db, block), F32),
        ),
        in_specs=[hbm, hbm, vmem, smem, vmem, smem, smem, vmem],
        out_specs=(vmem, vmem),
        scratch_shapes=[
            pltpu.VMEM((2, local_width, total_cols), BF16),
            pltpu.VMEM((chunks, total_cols, width), BF16),
            pltpu.VMEM((chunks, devices, 2 * width, local_width), BF16),
            pltpu.VMEM((2, devices, local_width, local_width), BF16),
            pltpu.VMEM((chunks, 2 * width, local_width), F32),
            pltpu.VMEM((chunks, poles, width, local_width), F32),
            pltpu.VMEM((2, total_cols, local_width), BF16),
            pltpu.VMEM((2, total_cols, local_width), BF16),
            pltpu.VMEM((total_cols, block), F32),
            pltpu.VMEM((2, zs * db, block), F32),
            pltpu.VMEM((2, zs, db, block), F32),
            pltpu.VMEM((2 * zs, db, block), F32),
            pltpu.VMEM((poles, db, block), F32),
            dma,
            dma,
            dma((chunks, devices)),
            dma((chunks, zs, 2)),
            dma((chunks, zs)),
            dma((chunks, zs)),
            dma((chunks, 2, zs)),
            dma((chunks, poles)),
            dma((chunks, poles)),
            dma((2,)),
            dma((2,)),
            dma((2 * zs,)),
            dma((2 * zs,)),
            dma((poles,)),
            dma((poles,)),
        ],
        compiler_params=pltpu.CompilerParams(
            collective_id=0, has_side_effects=True, vmem_limit_bytes=60 * 1024 * 1024
        ),
    )(
        factor[0],
        inverse[0].reshape(2, devices, local_width, local_width),
        diag_inverse[0],
        widths,
        pattern.T,
        owner,
        assign,
        pole_weights.T,
    )


def solution(mesh):
    placed = (
        P("pole", None, None, ("row", "col")),
        P("pole", None, ("row", "col"), None),
        P("pole", None, ("row", "col"), None),
        P(),
        P(),
        P(),
        P("pole"),
        P(),
    )
    return jax.shard_map(
        local,
        mesh=mesh,
        in_specs=placed,
        out_specs=(P(("row", "col"), None), P(("row", "col"), None)),
        check_vma=False,
    )
```

```python
import functools

import jax
import jax.numpy as jnp
from jax import lax
from jax.experimental import pallas as pl
from jax.experimental.pallas import tpu as pltpu
from jax.sharding import PartitionSpec as P

F32 = jnp.float32
BF16 = jnp.bfloat16
MESH = pl.DeviceIdType.MESH


def dot(left, right):
    return jnp.dot(left, right, preferred_element_type=F32)


def dot_nt(left, right):
    return lax.dot_general(left, right, (((1,), (1,)), ((), ())), preferred_element_type=F32)


def kernel(
    dims,
    factor_ref,
    inv_ref,
    dinv_ref,
    widths_ref,
    pattern_ref,
    owner_ref,
    assign_ref,
    weights_ref,
    panel_ref,
    diag_ref,
    factor,
    place_ref,
    pieces,
    inv,
    acc,
    shares,
    xe,
    le,
    gram,
    half,
    half_sum,
    parts,
    totals,
    factor_sem,
    inv_sem,
    recv,
    sz,
    sx,
    sc,
    ys,
    yr,
    d1s,
    d1r,
    d2s,
    d2r,
    d3s,
    d3r,
):
    chunks, zs, poles, width, blocks_k, block, db = dims
    pole = lax.axis_index("pole")
    row = lax.axis_index("row")
    z = lax.axis_index("col")
    hi = row // 2
    lo = row % 2
    sibling = hi * 2 + (1 - lo)
    across = (1 - hi) * 2 + lo

    def at(h, l, zz):
        return (h * 2 + l) * zs + zz

    me = at(hi, lo, z)
    mine = hi * zs + z

    barrier = pltpu.get_barrier_semaphore()
    pl.semaphore_signal(
        barrier, inc=1, device_id=(pole, sibling, z), device_id_type=MESH
    )

    @pl.loop(0, 2 * zs)
    def _(j):
        @pl.when(j != mine)
        def _():
            pl.semaphore_signal(
                barrier,
                inc=1,
                device_id=(pole, (j // zs) * 2 + lo, j % zs),
                device_id_type=MESH,
            )

    @pl.loop(0, poles)
    def _(p):
        @pl.when(p != pole)
        def _():
            pl.semaphore_signal(
                barrier, inc=1, device_id=(p, row, z), device_id_type=MESH
            )

    fetch = pltpu.make_async_copy(factor_ref, factor, factor_sem)
    fetch.start()
    load = pltpu.make_async_copy(inv_ref, inv, inv_sem)
    load.start()

    live = chunks * width
    lt_width = inv.shape[3]
    local_width = factor.shape[1]
    starts = [jnp.int32(0)]
    for k in range(1, blocks_k):
        starts.append(starts[-1] + widths_ref[k - 1])
    slot = lax.broadcasted_iota(jnp.int32, (live, block), 0)
    position = lax.broadcasted_iota(jnp.int32, (live, block), 1)

    fetch.wait()
    for i in range(local_width // block):
        rows = slice(i * block, (i + 1) * block)
        found = [jnp.zeros((live, block), F32)] * 2
        here = lax.broadcasted_iota(jnp.int32, pattern_ref.shape, 1)
        here = here == me * (local_width // block) + i
        kinds = jnp.sum(jnp.where(here, pattern_ref[...], 0), axis=1, keepdims=True)
        for k in range(blocks_k):
            kept = widths_ref[k] * kinds[k : k + 1]
            hit = (slot == position + starts[k]) & (position < kept)
            pick = jnp.where(hit, 1.0, 0.0).astype(BF16)
            for part in range(2):
                found[part] += dot_nt(pick, factor[part, rows, k * block : (k + 1) * block])
        for part in range(2):
            packed = found[part].astype(BF16).reshape(chunks, width, block)
            pieces[:, me, part * width : (part + 1) * width, rows] = packed
    pl.semaphore_wait(barrier, 1 + (2 * zs - 1) + (poles - 1))

    def send(c, q, send_sem, to_row, to_col):
        return pltpu.make_async_remote_copy(
            src_ref=pieces.at[c, q],
            dst_ref=pieces.at[c, q],
            send_sem=send_sem,
            recv_sem=recv.at[c, q],
            device_id=(pole, to_row, to_col),
            device_id_type=MESH,
        )

    def up(c, zz):
        return send(c, at(hi, lo, zz), sz.at[c, zz, 1], row, z + 1)

    def down(c, zz):
        return send(c, at(hi, lo, zz), sz.at[c, zz, 0], row, z - 1)

    def cross(c, zz):
        return send(c, at(hi, lo, zz), sx.at[c, zz], across, z)

    def over(c, h, zz):
        return send(c, at(h, lo, zz), sc.at[c, h, zz], sibling, z)

    def arrived(c, q):
        send(c, q, sx.at[0, 0], across, z).wait_recv()

    def goes_up(zz):
        return (zz <= z) & (z < zs - 1)

    def goes_down(zz):
        return (zz >= z) & (z > 0)

    def along(visit_up, visit_down, zz):
        @pl.when(goes_up(zz))
        def _():
            visit_up()

        @pl.when(goes_down(zz))
        def _():
            visit_down()

    def forward(c, zz):
        along(lambda: up(c, zz).start(), lambda: down(c, zz).start(), zz)
        cross(c, zz).start()
        over(c, hi, zz).start()

    @pl.loop(0, chunks)
    def _(c):
        forward(c, z)

    source = lax.broadcasted_iota(jnp.int32, (block, width), 0)
    target = lax.broadcasted_iota(jnp.int32, (block, width), 1)

    @pl.loop(0, chunks)
    def _(c):
        for k in range(blocks_k):
            hit = (target + c * width == source + starts[k]) & (source < widths_ref[k])
            place_ref[c, k * block : (k + 1) * block] = jnp.where(hit, 1.0, 0.0).astype(BF16)

    acc[...] = jnp.zeros_like(acc)
    xe[...] = jnp.zeros_like(xe)
    le[...] = jnp.zeros_like(le)
    panel_ref[...] = jnp.zeros_like(panel_ref)
    load.wait()

    def compute(pair, q):
        some = pl.ds(2 * pair, 2)
        lt = pieces[some, q].reshape(4 * width, lt_width)
        u = dot(lt, inv[0, q]).reshape(2, 2 * width, lt_width)
        v = dot(lt, inv[1, q]).reshape(2, 2 * width, lt_width)
        acc[some, :width] += u[:, :width] - v[:, width:]
        acc[some, width:] += u[:, width:] + v[:, :width]

    def share(c, p):
        return pltpu.make_async_remote_copy(
            src_ref=shares.at[c, pole],
            dst_ref=shares.at[c, pole],
            send_sem=ys.at[c, p],
            recv_sem=yr.at[c, pole],
            device_id=(p, row, z),
            device_id_type=MESH,
        )

    def share_from(c, p):
        return pltpu.make_async_remote_copy(
            src_ref=shares.at[c, p],
            dst_ref=shares.at[c, p],
            send_sem=ys.at[c, p],
            recv_sem=yr.at[c, p],
            device_id=(p, row, z),
            device_id_type=MESH,
        )

    chosen = lax.broadcasted_iota(jnp.int32, weights_ref.shape, 1) == assign_ref[0]
    weight = jnp.sum(jnp.where(chosen, weights_ref[...], 0.0), axis=1, keepdims=True)
    wr = weight[0:1]
    wi = weight[1:2]

    def others(visit):
        @pl.loop(0, poles)
        def _(p):
            @pl.when(p != pole)
            def _():
                visit(p)

    def finish(c):
        xr = -acc[c, :width]
        xi = -acc[c, width:]
        shares[c, pole] = wr * xi + wi * xr
        others(lambda p: share(c, p).start())
        place = place_ref[c]
        xe[0] += dot(place, xr.astype(BF16)).astype(BF16)
        xe[1] += dot(place, xi.astype(BF16)).astype(BF16)

    def receive(c):
        others(lambda p: share_from(c, p).wait_recv())
        total = shares[c, 0]
        for p in range(1, poles):
            total = total + shares[c, p]
        total = total.T
        top = total.astype(BF16)
        rest = total - top.astype(F32)
        middle = rest.astype(BF16)
        low = (rest - middle.astype(F32)).astype(BF16)
        place = place_ref[c]
        terms = jnp.concatenate([top, middle, low], axis=1)
        panel_ref[...] += dot_nt(terms, jnp.concatenate([place] * 3, axis=1))

    pairs = chunks // 2
    slots = pairs * zs
    near, far = 2, 3

    @pl.loop(0, slots + far)
    def _(n):
        @pl.loop(0, 2)
        def _(side):
            def visit(m, body):
                s = m // pairs
                zz = jnp.where(side == 0, z - s, z + s)
                inside = (m >= 0) & (m < slots) & (zz >= 0) & (zz < zs)

                @pl.when(inside & ((s > 0) | (side == 0)))
                def _():
                    body(lax.rem(m, pairs), zz)

            def first(pair, zz):
                @pl.when(zz != z)
                def _():
                    for c in (2 * pair, 2 * pair + 1):
                        arrived(c, at(hi, lo, zz))
                        forward(c, zz)

                compute(pair, at(hi, lo, zz))

            def second(pair, zz):
                for c in (2 * pair, 2 * pair + 1):
                    arrived(c, at(1 - hi, lo, zz))
                    over(c, 1 - hi, zz).start()
                    arrived(c, at(hi, 1 - lo, zz))
                compute(pair, at(hi, 1 - lo, zz))
                compute(pair, at(1 - hi, lo, zz))

            def third(pair, zz):
                for c in (2 * pair, 2 * pair + 1):
                    arrived(c, at(1 - hi, 1 - lo, zz))
                compute(pair, at(1 - hi, 1 - lo, zz))

            visit(n, first)
            visit(n - near, second)
            visit(n - far, third)

        @pl.when(n - far >= slots - pairs)
        def _():
            pair = lax.rem(n - far, pairs)
            finish(2 * pair)
            finish(2 * pair + 1)

    @pl.loop(0, chunks)
    def _(c):
        lt = pieces[c, owner_ref[me]]
        place = place_ref[c]
        le[0] += dot(place, lt[:width]).astype(BF16)
        le[1] += dot(place, lt[width:]).astype(BF16)

    for k in range(blocks_k):
        rows = slice(k * block, (k + 1) * block)
        lr, li, xr, xi = le[0, rows], le[1, rows], xe[0, rows], xe[1, rows]
        real = dot_nt(lr, xr) - dot_nt(li, xi)
        imag = dot_nt(lr, xi) + dot_nt(li, xr)
        gram[rows] = wr * imag + wi * real

    span = zs * db

    def rows_of(h, l):
        return pl.ds(pl.multiple_of((h * 2 + l) * span, 8), span)

    halves = []
    for h in range(2):
        halves.append(
            pltpu.make_async_remote_copy(
                src_ref=gram.at[rows_of(h, 1 - lo)],
                dst_ref=half.at[h],
                send_sem=d1s.at[h],
                recv_sem=d1r.at[h],
                device_id=(pole, sibling, z),
                device_id_type=MESH,
            )
        )
        halves[h].start()

    @pl.loop(0, chunks - 1)
    def _(c):
        receive(c)

    for h in range(2):
        halves[h].wait_recv()
        half_sum[h] = (gram[rows_of(h, lo)] + half[h]).reshape(zs, db, block)

    def part(j):
        return pltpu.make_async_remote_copy(
            src_ref=half_sum.at[j // zs, j % zs],
            dst_ref=parts.at[mine],
            send_sem=d2s.at[j],
            recv_sem=d2r.at[mine],
            device_id=(pole, (j // zs) * 2 + lo, j % zs),
            device_id_type=MESH,
        )

    def part_from(j):
        return pltpu.make_async_remote_copy(
            src_ref=parts.at[j],
            dst_ref=parts.at[j],
            send_sem=d2s.at[j],
            recv_sem=d2r.at[j],
            device_id=(pole, (j // zs) * 2 + lo, j % zs),
            device_id_type=MESH,
        )

    def peers(visit):
        @pl.loop(0, 2 * zs)
        def _(j):
            @pl.when(j != mine)
            def _():
                visit(j)

    peers(lambda j: part(j).start())
    parts[mine] = half_sum[hi, z]
    receive(chunks - 1)
    peers(lambda j: part_from(j).wait_recv())
    total = parts[0]
    for j in range(1, 2 * zs):
        total = total + parts[j]
    dinv = dinv_ref[...].astype(F32)
    totals[pole] = (wr * dinv[1] + wi * dinv[0]) - total

    def result(p, slot):
        return pltpu.make_async_remote_copy(
            src_ref=totals.at[slot],
            dst_ref=totals.at[slot],
            send_sem=d3s.at[p],
            recv_sem=d3r.at[slot],
            device_id=(p, row, z),
            device_id_type=MESH,
        )

    others(lambda p: result(p, pole).start())

    @pl.loop(0, chunks)
    def _(c):
        @pl.loop(0, zs)
        def _(zz):
            over(c, 0, zz).wait_send()
            over(c, 1, zz).wait_send()

            cross(c, zz).wait_send()

            along(lambda: up(c, zz).wait_send(), lambda: down(c, zz).wait_send(), zz)

        others(lambda p: share(c, p).wait_send())

    for h in range(2):
        halves[h].wait_send()
    peers(lambda j: part(j).wait_send())
    others(lambda p: result(p, p).wait_recv())
    final = totals[0]
    for p in range(1, poles):
        final = final + totals[p]
    diag_ref[...] = final
    others(lambda p: result(p, pole).wait_send())


def local(inverse, factor, diag_inverse, widths, pattern, owner, assign, pole_weights):
    zs = lax.axis_size("col")
    poles = lax.axis_size("pole")
    rows_n = lax.axis_size("row")
    assert rows_n == 4
    devices = rows_n * zs
    local_width = factor.shape[2]
    total_cols = factor.shape[3]
    db = diag_inverse.shape[2]
    block = diag_inverse.shape[3]
    blocks_k = total_cols // block
    live = 2 * total_cols // 3
    width = 128
    chunks = live // width

    dims = (chunks, zs, poles, width, blocks_k, block, db)
    vmem = pl.BlockSpec(memory_space=pltpu.VMEM)
    hbm = pl.BlockSpec(memory_space=pl.ANY)
    smem = pl.BlockSpec(memory_space=pltpu.SMEM)
    dma = pltpu.SemaphoreType.DMA
    return pl.pallas_call(
        functools.partial(kernel, dims),
        out_shape=(
            jax.ShapeDtypeStruct((local_width, total_cols), F32),
            jax.ShapeDtypeStruct((db, block), F32),
        ),
        in_specs=[hbm, hbm, vmem, smem, vmem, smem, smem, vmem],
        out_specs=(vmem, vmem),
        scratch_shapes=[
            pltpu.VMEM((2, local_width, total_cols), BF16),
            pltpu.VMEM((chunks, total_cols, width), BF16),
            pltpu.VMEM((chunks, devices, 2 * width, local_width), BF16),
            pltpu.VMEM((2, devices, local_width, local_width), BF16),
            pltpu.VMEM((chunks, 2 * width, local_width), F32),
            pltpu.VMEM((chunks, poles, width, local_width), F32),
            pltpu.VMEM((2, total_cols, local_width), BF16),
            pltpu.VMEM((2, total_cols, local_width), BF16),
            pltpu.VMEM((total_cols, block), F32),
            pltpu.VMEM((2, zs * db, block), F32),
            pltpu.VMEM((2, zs, db, block), F32),
            pltpu.VMEM((2 * zs, db, block), F32),
            pltpu.VMEM((poles, db, block), F32),
            dma,
            dma,
            dma((chunks, devices)),
            dma((chunks, zs, 2)),
            dma((chunks, zs)),
            dma((chunks, 2, zs)),
            dma((chunks, poles)),
            dma((chunks, poles)),
            dma((2,)),
            dma((2,)),
            dma((2 * zs,)),
            dma((2 * zs,)),
            dma((poles,)),
            dma((poles,)),
        ],
        compiler_params=pltpu.CompilerParams(
            collective_id=0, has_side_effects=True, vmem_limit_bytes=60 * 1024 * 1024
        ),
    )(
        factor[0],
        inverse[0].reshape(2, devices, local_width, local_width),
        diag_inverse[0],
        widths,
        pattern.T,
        owner,
        assign,
        pole_weights.T,
    )


def solution(mesh):
    placed = (
        P("pole", None, None, ("row", "col")),
        P("pole", None, ("row", "col"), None),
        P("pole", None, ("row", "col"), None),
        P(),
        P(),
        P(),
        P("pole"),
        P(),
    )
    return jax.shard_map(
        local,
        mesh=mesh,
        in_specs=placed,
        out_specs=(P(("row", "col"), None), P(("row", "col"), None)),
        check_vma=False,
    )
```

```python
import functools

import jax
import jax.numpy as jnp
from jax import lax
from jax.experimental import pallas as pl
from jax.experimental.pallas import tpu as pltpu
from jax.sharding import PartitionSpec as P

F32 = jnp.float32
BF16 = jnp.bfloat16
MESH = pl.DeviceIdType.MESH


def dot(left, right):
    return jnp.dot(left, right, preferred_element_type=F32)


def dot_nt(left, right):
    return lax.dot_general(left, right, (((1,), (1,)), ((), ())), preferred_element_type=F32)


def kernel(
    dims,
    factor_ref,
    inv_ref,
    dinv_ref,
    widths_ref,
    pattern_ref,
    owner_ref,
    assign_ref,
    weights_ref,
    panel_ref,
    diag_ref,
    factor,
    place_ref,
    pieces,
    inv,
    acc,
    held,
    shares,
    xe,
    le,
    gram,
    half,
    half_sum,
    parts,
    totals,
    factor_sem,
    inv_sem,
    recv,
    sz,
    sx,
    sc,
    ys,
    yr,
    d1s,
    d1r,
    d2s,
    d2r,
    d3s,
    d3r,
):
    chunks, zs, poles, width, blocks_k, block, db = dims
    pole = lax.axis_index("pole")
    row = lax.axis_index("row")
    z = lax.axis_index("col")
    hi = row // 2
    lo = row % 2
    sibling = hi * 2 + (1 - lo)
    across = (1 - hi) * 2 + lo

    def at(h, l, zz):
        return (h * 2 + l) * zs + zz

    me = at(hi, lo, z)
    mine = hi * zs + z

    barrier = pltpu.get_barrier_semaphore()
    pl.semaphore_signal(
        barrier, inc=1, device_id=(pole, sibling, z), device_id_type=MESH
    )

    @pl.loop(0, 2 * zs)
    def _(j):
        @pl.when(j != mine)
        def _():
            pl.semaphore_signal(
                barrier,
                inc=1,
                device_id=(pole, (j // zs) * 2 + lo, j % zs),
                device_id_type=MESH,
            )

    @pl.loop(0, poles)
    def _(p):
        @pl.when(p != pole)
        def _():
            pl.semaphore_signal(
                barrier, inc=1, device_id=(p, row, z), device_id_type=MESH
            )

    fetch = pltpu.make_async_copy(factor_ref, factor, factor_sem)
    fetch.start()
    load = pltpu.make_async_copy(inv_ref, inv, inv_sem)
    load.start()

    live = chunks * width
    local_width = factor.shape[1]
    starts = [jnp.int32(0)]
    for k in range(1, blocks_k):
        starts.append(starts[-1] + widths_ref[k - 1])
    slot = lax.broadcasted_iota(jnp.int32, (live, block), 0)
    position = lax.broadcasted_iota(jnp.int32, (live, block), 1)

    fetch.wait()
    for i in range(local_width // block):
        rows = slice(i * block, (i + 1) * block)
        found = [jnp.zeros((live, block), F32)] * 2
        here = lax.broadcasted_iota(jnp.int32, pattern_ref.shape, 1)
        here = here == me * (local_width // block) + i
        kinds = jnp.sum(jnp.where(here, pattern_ref[...], 0), axis=1, keepdims=True)
        for k in range(blocks_k):
            kept = widths_ref[k] * kinds[k : k + 1]
            hit = (slot == position + starts[k]) & (position < kept)
            pick = jnp.where(hit, 1.0, 0.0).astype(BF16)
            for part in range(2):
                found[part] += dot_nt(pick, factor[part, rows, k * block : (k + 1) * block])
        for part in range(2):
            packed = found[part].astype(BF16).reshape(chunks, width, block)
            pieces[:, me, part * width : (part + 1) * width, rows] = packed
    pl.semaphore_wait(barrier, 1 + (2 * zs - 1) + (poles - 1))

    def send(c, q, send_sem, to_row, to_col):
        return pltpu.make_async_remote_copy(
            src_ref=pieces.at[c, q],
            dst_ref=pieces.at[c, q],
            send_sem=send_sem,
            recv_sem=recv.at[c, q],
            device_id=(pole, to_row, to_col),
            device_id_type=MESH,
        )

    def up(c, zz):
        return send(c, at(hi, lo, zz), sz.at[c, zz, 1], row, z + 1)

    def down(c, zz):
        return send(c, at(hi, lo, zz), sz.at[c, zz, 0], row, z - 1)

    def cross(c, zz):
        return send(c, at(hi, lo, zz), sx.at[c, zz], across, z)

    def over(c, h, zz):
        return send(c, at(h, lo, zz), sc.at[c, h, zz], sibling, z)

    def arrived(c, q):
        send(c, q, sx.at[0, 0], across, z).wait_recv()

    def goes_up(zz):
        return (zz <= z) & (z < zs - 1)

    def goes_down(zz):
        return (zz >= z) & (z > 0)

    def along(visit_up, visit_down, zz):
        @pl.when(goes_up(zz))
        def _():
            visit_up()

        @pl.when(goes_down(zz))
        def _():
            visit_down()

    def forward(c, zz):
        along(lambda: up(c, zz).start(), lambda: down(c, zz).start(), zz)
        cross(c, zz).start()
        over(c, hi, zz).start()

    for c in range(min(2, chunks)):
        forward(c, z)

    source = lax.broadcasted_iota(jnp.int32, (block, width), 0)
    target = lax.broadcasted_iota(jnp.int32, (block, width), 1)

    @pl.loop(0, chunks)
    def _(c):
        for k in range(blocks_k):
            hit = (target + c * width == source + starts[k]) & (source < widths_ref[k])
            place_ref[c, k * block : (k + 1) * block] = jnp.where(hit, 1.0, 0.0).astype(BF16)

    acc[...] = jnp.zeros_like(acc)
    held[...] = jnp.zeros_like(held)
    xe[...] = jnp.zeros_like(xe)
    le[...] = jnp.zeros_like(le)
    panel_ref[...] = jnp.zeros_like(panel_ref)
    load.wait()

    def compute(c, q):
        lt = pieces[c, q]
        held[c] = jnp.where(q == owner_ref[me], lt, held[c])
        u = dot(lt, inv[0, q])
        v = dot(lt, inv[1, q])
        acc[c, :width] += u[:width] - v[width:]
        acc[c, width:] += u[width:] + v[:width]

    def share(c, p):
        return pltpu.make_async_remote_copy(
            src_ref=shares.at[c, pole],
            dst_ref=shares.at[c, pole],
            send_sem=ys.at[c, p],
            recv_sem=yr.at[c, pole],
            device_id=(p, row, z),
            device_id_type=MESH,
        )

    def share_from(c, p):
        return pltpu.make_async_remote_copy(
            src_ref=shares.at[c, p],
            dst_ref=shares.at[c, p],
            send_sem=ys.at[c, p],
            recv_sem=yr.at[c, p],
            device_id=(p, row, z),
            device_id_type=MESH,
        )

    chosen = lax.broadcasted_iota(jnp.int32, weights_ref.shape, 1) == assign_ref[0]
    weight = jnp.sum(jnp.where(chosen, weights_ref[...], 0.0), axis=1, keepdims=True)
    wr = weight[0:1]
    wi = weight[1:2]

    def others(visit):
        @pl.loop(0, poles)
        def _(p):
            @pl.when(p != pole)
            def _():
                visit(p)

    def finish(c):
        xr = -acc[c, :width]
        xi = -acc[c, width:]
        shares[c, pole] = wr * xi + wi * xr
        others(lambda p: share(c, p).start())
        place = place_ref[c]
        xe[0] += dot(place, xr.astype(BF16)).astype(BF16)
        xe[1] += dot(place, xi.astype(BF16)).astype(BF16)
        le[0] += dot(place, held[c, :width]).astype(BF16)
        le[1] += dot(place, held[c, width:]).astype(BF16)

    def receive(c):
        others(lambda p: share_from(c, p).wait_recv())
        total = shares[c, 0]
        for p in range(1, poles):
            total = total + shares[c, p]
        total = total.T
        top = total.astype(BF16)
        rest = total - top.astype(F32)
        middle = rest.astype(BF16)
        low = (rest - middle.astype(F32)).astype(BF16)
        place = place_ref[c]
        terms = jnp.concatenate([top, middle, low], axis=1)
        panel_ref[...] += dot_nt(terms, jnp.concatenate([place] * 3, axis=1))

    @pl.loop(0, chunks + 2)
    def _(t):
        @pl.when(t < chunks - 2)
        def _():
            forward(t + 2, z)

        @pl.when(t >= 4)
        def _():
            receive(t - 4)

        @pl.loop(0, 2 * zs)
        def _(j):
            s = j // 2
            zz = jnp.where(j % 2 == 0, z - s, z + s)

            @pl.when((zz >= 0) & (zz < zs) & (j != 1))
            def _():
                @pl.when(t < chunks)
                def _():
                    @pl.when(zz != z)
                    def _():
                        arrived(t, at(hi, lo, zz))
                        forward(t, zz)

                    compute(t, at(hi, lo, zz))

                @pl.when((t >= 1) & (t <= chunks))
                def _():
                    arrived(t - 1, at(1 - hi, lo, zz))
                    over(t - 1, 1 - hi, zz).start()
                    arrived(t - 1, at(hi, 1 - lo, zz))
                    compute(t - 1, at(hi, 1 - lo, zz))
                    compute(t - 1, at(1 - hi, lo, zz))

                @pl.when(t >= 2)
                def _():
                    arrived(t - 2, at(1 - hi, 1 - lo, zz))
                    compute(t - 2, at(1 - hi, 1 - lo, zz))

        @pl.when(t >= 2)
        def _():
            finish(t - 2)

    for k in range(blocks_k):
        rows = slice(k * block, (k + 1) * block)
        lr, li, xr, xi = le[0, rows], le[1, rows], xe[0, rows], xe[1, rows]
        real = dot_nt(lr, xr) - dot_nt(li, xi)
        imag = dot_nt(lr, xi) + dot_nt(li, xr)
        gram[rows] = wr * imag + wi * real

    span = zs * db

    def rows_of(h, l):
        return pl.ds(pl.multiple_of((h * 2 + l) * span, 8), span)

    halves = []
    for h in range(2):
        halves.append(
            pltpu.make_async_remote_copy(
                src_ref=gram.at[rows_of(h, 1 - lo)],
                dst_ref=half.at[h],
                send_sem=d1s.at[h],
                recv_sem=d1r.at[h],
                device_id=(pole, sibling, z),
                device_id_type=MESH,
            )
        )
        halves[h].start()

    receive(chunks - 2)

    for h in range(2):
        halves[h].wait_recv()
        half_sum[h] = (gram[rows_of(h, lo)] + half[h]).reshape(zs, db, block)

    def part(j):
        return pltpu.make_async_remote_copy(
            src_ref=half_sum.at[j // zs, j % zs],
            dst_ref=parts.at[mine],
            send_sem=d2s.at[j],
            recv_sem=d2r.at[mine],
            device_id=(pole, (j // zs) * 2 + lo, j % zs),
            device_id_type=MESH,
        )

    def part_from(j):
        return pltpu.make_async_remote_copy(
            src_ref=parts.at[j],
            dst_ref=parts.at[j],
            send_sem=d2s.at[j],
            recv_sem=d2r.at[j],
            device_id=(pole, (j // zs) * 2 + lo, j % zs),
            device_id_type=MESH,
        )

    def peers(visit):
        @pl.loop(0, 2 * zs)
        def _(j):
            @pl.when(j != mine)
            def _():
                visit(j)

    peers(lambda j: part(j).start())
    parts[mine] = half_sum[hi, z]
    receive(chunks - 1)
    peers(lambda j: part_from(j).wait_recv())
    total = parts[0]
    for j in range(1, 2 * zs):
        total = total + parts[j]
    dinv = dinv_ref[...].astype(F32)
    totals[pole] = (wr * dinv[1] + wi * dinv[0]) - total

    def result(p, slot):
        return pltpu.make_async_remote_copy(
            src_ref=totals.at[slot],
            dst_ref=totals.at[slot],
            send_sem=d3s.at[p],
            recv_sem=d3r.at[slot],
            device_id=(p, row, z),
            device_id_type=MESH,
        )

    others(lambda p: result(p, pole).start())

    @pl.loop(0, chunks)
    def _(c):
        @pl.loop(0, zs)
        def _(zz):
            over(c, 0, zz).wait_send()
            over(c, 1, zz).wait_send()

            cross(c, zz).wait_send()

            along(lambda: up(c, zz).wait_send(), lambda: down(c, zz).wait_send(), zz)

        others(lambda p: share(c, p).wait_send())

    for h in range(2):
        halves[h].wait_send()
    peers(lambda j: part(j).wait_send())
    others(lambda p: result(p, p).wait_recv())
    final = totals[0]
    for p in range(1, poles):
        final = final + totals[p]
    diag_ref[...] = final
    others(lambda p: result(p, pole).wait_send())


def local(inverse, factor, diag_inverse, widths, pattern, owner, assign, pole_weights):
    zs = lax.axis_size("col")
    poles = lax.axis_size("pole")
    rows_n = lax.axis_size("row")
    assert rows_n == 4
    devices = rows_n * zs
    local_width = factor.shape[2]
    total_cols = factor.shape[3]
    db = diag_inverse.shape[2]
    block = diag_inverse.shape[3]
    blocks_k = total_cols // block
    live = 2 * total_cols // 3
    width = 128
    chunks = live // width

    dims = (chunks, zs, poles, width, blocks_k, block, db)
    vmem = pl.BlockSpec(memory_space=pltpu.VMEM)
    hbm = pl.BlockSpec(memory_space=pl.ANY)
    smem = pl.BlockSpec(memory_space=pltpu.SMEM)
    dma = pltpu.SemaphoreType.DMA
    return pl.pallas_call(
        functools.partial(kernel, dims),
        out_shape=(
            jax.ShapeDtypeStruct((local_width, total_cols), F32),
            jax.ShapeDtypeStruct((db, block), F32),
        ),
        in_specs=[hbm, hbm, vmem, smem, vmem, smem, smem, vmem],
        out_specs=(vmem, vmem),
        scratch_shapes=[
            pltpu.VMEM((2, local_width, total_cols), BF16),
            pltpu.VMEM((chunks, total_cols, width), BF16),
            pltpu.VMEM((chunks, devices, 2 * width, local_width), BF16),
            pltpu.VMEM((2, devices, local_width, local_width), BF16),
            pltpu.VMEM((chunks, 2 * width, local_width), F32),
            pltpu.VMEM((chunks, 2 * width, local_width), BF16),
            pltpu.VMEM((chunks, poles, width, local_width), F32),
            pltpu.VMEM((2, total_cols, local_width), BF16),
            pltpu.VMEM((2, total_cols, local_width), BF16),
            pltpu.VMEM((total_cols, block), F32),
            pltpu.VMEM((2, zs * db, block), F32),
            pltpu.VMEM((2, zs, db, block), F32),
            pltpu.VMEM((2 * zs, db, block), F32),
            pltpu.VMEM((poles, db, block), F32),
            dma,
            dma,
            dma((chunks, devices)),
            dma((chunks, zs, 2)),
            dma((chunks, zs)),
            dma((chunks, 2, zs)),
            dma((chunks, poles)),
            dma((chunks, poles)),
            dma((2,)),
            dma((2,)),
            dma((2 * zs,)),
            dma((2 * zs,)),
            dma((poles,)),
            dma((poles,)),
        ],
        compiler_params=pltpu.CompilerParams(
            collective_id=0, has_side_effects=True, vmem_limit_bytes=60 * 1024 * 1024
        ),
    )(
        factor[0],
        inverse[0].reshape(2, devices, local_width, local_width),
        diag_inverse[0],
        widths,
        pattern.T,
        owner,
        assign,
        pole_weights.T,
    )


def solution(mesh):
    placed = (
        P("pole", None, None, ("row", "col")),
        P("pole", None, ("row", "col"), None),
        P("pole", None, ("row", "col"), None),
        P(),
        P(),
        P(),
        P("pole"),
        P(),
    )
    return jax.shard_map(
        local,
        mesh=mesh,
        in_specs=placed,
        out_specs=(P(("row", "col"), None), P(("row", "col"), None)),
        check_vma=False,
    )
```

```python
import functools

import jax
import jax.numpy as jnp
from jax import lax
from jax.experimental import pallas as pl
from jax.experimental.pallas import tpu as pltpu
from jax.sharding import PartitionSpec as P

F32 = jnp.float32
BF16 = jnp.bfloat16
MESH = pl.DeviceIdType.MESH


def dot(left, right):
    return jnp.dot(left, right, preferred_element_type=F32)


def dot_nt(left, right):
    return lax.dot_general(left, right, (((1,), (1,)), ((), ())), preferred_element_type=F32)


def kernel(
    dims,
    factor_ref,
    inv_ref,
    dinv_ref,
    widths_ref,
    pattern_ref,
    owner_ref,
    assign_ref,
    weights_ref,
    panel_ref,
    diag_ref,
    factor,
    place_ref,
    pieces,
    inv,
    acc,
    held,
    shares,
    xe,
    le,
    gram,
    half,
    half_sum,
    parts,
    totals,
    factor_sem,
    inv_sem,
    recv,
    sz,
    sx,
    sc,
    ys,
    yr,
    d1s,
    d1r,
    d2s,
    d2r,
    d3s,
    d3r,
):
    chunks, zs, poles, width, blocks_k, block, db = dims
    pole = lax.axis_index("pole")
    row = lax.axis_index("row")
    z = lax.axis_index("col")
    hi = row // 2
    lo = row % 2
    sibling = hi * 2 + (1 - lo)
    across = (1 - hi) * 2 + lo

    def at(h, l, zz):
        return (h * 2 + l) * zs + zz

    me = at(hi, lo, z)
    mine = hi * zs + z

    barrier = pltpu.get_barrier_semaphore()
    pl.semaphore_signal(
        barrier, inc=1, device_id=(pole, sibling, z), device_id_type=MESH
    )

    @pl.loop(0, 2 * zs)
    def _(j):
        @pl.when(j != mine)
        def _():
            pl.semaphore_signal(
                barrier,
                inc=1,
                device_id=(pole, (j // zs) * 2 + lo, j % zs),
                device_id_type=MESH,
            )

    @pl.loop(0, poles)
    def _(p):
        @pl.when(p != pole)
        def _():
            pl.semaphore_signal(
                barrier, inc=1, device_id=(p, row, z), device_id_type=MESH
            )

    fetch = pltpu.make_async_copy(factor_ref, factor, factor_sem)
    fetch.start()
    load = pltpu.make_async_copy(inv_ref, inv, inv_sem)
    load.start()

    live = chunks * width
    local_width = factor.shape[1]
    starts = [jnp.int32(0)]
    for k in range(1, blocks_k):
        starts.append(starts[-1] + widths_ref[k - 1])
    slot = lax.broadcasted_iota(jnp.int32, (live, block), 0)
    position = lax.broadcasted_iota(jnp.int32, (live, block), 1)

    fetch.wait()
    for i in range(local_width // block):
        rows = slice(i * block, (i + 1) * block)
        found = [jnp.zeros((live, block), F32)] * 2
        here = lax.broadcasted_iota(jnp.int32, pattern_ref.shape, 1)
        here = here == me * (local_width // block) + i
        kinds = jnp.sum(jnp.where(here, pattern_ref[...], 0), axis=1, keepdims=True)
        for k in range(blocks_k):
            kept = widths_ref[k] * kinds[k : k + 1]
            hit = (slot == position + starts[k]) & (position < kept)
            pick = jnp.where(hit, 1.0, 0.0).astype(BF16)
            for part in range(2):
                found[part] += dot_nt(pick, factor[part, rows, k * block : (k + 1) * block])
        for part in range(2):
            packed = found[part].astype(BF16).reshape(chunks, width, block)
            pieces[:, me, part * width : (part + 1) * width, rows] = packed
    pl.semaphore_wait(barrier, 1 + (2 * zs - 1) + (poles - 1))

    def send(c, q, send_sem, to_row, to_col):
        return pltpu.make_async_remote_copy(
            src_ref=pieces.at[c, q],
            dst_ref=pieces.at[c, q],
            send_sem=send_sem,
            recv_sem=recv.at[c, q],
            device_id=(pole, to_row, to_col),
            device_id_type=MESH,
        )

    def up(c, zz):
        return send(c, at(hi, lo, zz), sz.at[c, zz, 1], row, z + 1)

    def down(c, zz):
        return send(c, at(hi, lo, zz), sz.at[c, zz, 0], row, z - 1)

    def cross(c, zz):
        return send(c, at(hi, lo, zz), sx.at[c, zz], across, z)

    def over(c, h, zz):
        return send(c, at(h, lo, zz), sc.at[c, h, zz], sibling, z)

    def arrived(c, q):
        send(c, q, sx.at[0, 0], across, z).wait_recv()

    def goes_up(zz):
        return (zz <= z) & (z < zs - 1)

    def goes_down(zz):
        return (zz >= z) & (z > 0)

    def along(visit_up, visit_down, zz):
        @pl.when(goes_up(zz))
        def _():
            visit_up()

        @pl.when(goes_down(zz))
        def _():
            visit_down()

    def forward(c, zz):
        along(lambda: up(c, zz).start(), lambda: down(c, zz).start(), zz)
        cross(c, zz).start()
        over(c, hi, zz).start()

    forward(0, z)

    source = lax.broadcasted_iota(jnp.int32, (block, width), 0)
    target = lax.broadcasted_iota(jnp.int32, (block, width), 1)

    @pl.loop(0, chunks)
    def _(c):
        for k in range(blocks_k):
            hit = (target + c * width == source + starts[k]) & (source < widths_ref[k])
            place_ref[c, k * block : (k + 1) * block] = jnp.where(hit, 1.0, 0.0).astype(BF16)

    acc[...] = jnp.zeros_like(acc)
    held[...] = jnp.zeros_like(held)
    xe[...] = jnp.zeros_like(xe)
    le[...] = jnp.zeros_like(le)
    panel_ref[...] = jnp.zeros_like(panel_ref)
    load.wait()

    def compute(c, q):
        lt = pieces[c, q]
        held[c] = jnp.where(q == owner_ref[me], lt, held[c])
        u = dot(lt, inv[0, q])
        v = dot(lt, inv[1, q])
        acc[c, :width] += u[:width] - v[width:]
        acc[c, width:] += u[width:] + v[:width]

    def share(c, p):
        return pltpu.make_async_remote_copy(
            src_ref=shares.at[c, pole],
            dst_ref=shares.at[c, pole],
            send_sem=ys.at[c, p],
            recv_sem=yr.at[c, pole],
            device_id=(p, row, z),
            device_id_type=MESH,
        )

    def share_from(c, p):
        return pltpu.make_async_remote_copy(
            src_ref=shares.at[c, p],
            dst_ref=shares.at[c, p],
            send_sem=ys.at[c, p],
            recv_sem=yr.at[c, p],
            device_id=(p, row, z),
            device_id_type=MESH,
        )

    chosen = lax.broadcasted_iota(jnp.int32, weights_ref.shape, 1) == assign_ref[0]
    weight = jnp.sum(jnp.where(chosen, weights_ref[...], 0.0), axis=1, keepdims=True)
    wr = weight[0:1]
    wi = weight[1:2]

    def others(visit):
        @pl.loop(0, poles)
        def _(p):
            @pl.when(p != pole)
            def _():
                visit(p)

    def finish(c):
        xr = -acc[c, :width]
        xi = -acc[c, width:]
        shares[c, pole] = wr * xi + wi * xr
        others(lambda p: share(c, p).start())
        place = place_ref[c]
        xe[0] += dot(place, xr.astype(BF16)).astype(BF16)
        xe[1] += dot(place, xi.astype(BF16)).astype(BF16)
        le[0] += dot(place, held[c, :width]).astype(BF16)
        le[1] += dot(place, held[c, width:]).astype(BF16)

    def receive(c):
        others(lambda p: share_from(c, p).wait_recv())
        total = shares[c, 0]
        for p in range(1, poles):
            total = total + shares[c, p]
        total = total.T
        top = total.astype(BF16)
        rest = total - top.astype(F32)
        middle = rest.astype(BF16)
        low = (rest - middle.astype(F32)).astype(BF16)
        place = place_ref[c]
        terms = jnp.concatenate([top, middle, low], axis=1)
        panel_ref[...] += dot_nt(terms, jnp.concatenate([place] * 3, axis=1))

    @pl.loop(0, chunks + 2)
    def _(t):
        @pl.when(t < chunks - 1)
        def _():
            forward(t + 1, z)

        @pl.when(t >= 4)
        def _():
            receive(t - 4)

        @pl.loop(0, 2 * zs)
        def _(j):
            s = j // 2
            zz = jnp.where(j % 2 == 0, z - s, z + s)

            @pl.when((zz >= 0) & (zz < zs) & (j != 1))
            def _():
                @pl.when(t < chunks)
                def _():
                    @pl.when(zz != z)
                    def _():
                        arrived(t, at(hi, lo, zz))
                        forward(t, zz)

                    compute(t, at(hi, lo, zz))

                @pl.when((t >= 1) & (t <= chunks))
                def _():
                    arrived(t - 1, at(1 - hi, lo, zz))
                    over(t - 1, 1 - hi, zz).start()
                    arrived(t - 1, at(hi, 1 - lo, zz))
                    compute(t - 1, at(hi, 1 - lo, zz))
                    compute(t - 1, at(1 - hi, lo, zz))

                @pl.when(t >= 2)
                def _():
                    arrived(t - 2, at(1 - hi, 1 - lo, zz))
                    compute(t - 2, at(1 - hi, 1 - lo, zz))

        @pl.when(t >= 2)
        def _():
            finish(t - 2)

    for k in range(blocks_k):
        rows = slice(k * block, (k + 1) * block)
        lr, li, xr, xi = le[0, rows], le[1, rows], xe[0, rows], xe[1, rows]
        real = dot_nt(lr, xr) - dot_nt(li, xi)
        imag = dot_nt(lr, xi) + dot_nt(li, xr)
        gram[rows] = wr * imag + wi * real

    span = zs * db

    def rows_of(h, l):
        return pl.ds(pl.multiple_of((h * 2 + l) * span, 8), span)

    halves = []
    for h in range(2):
        halves.append(
            pltpu.make_async_remote_copy(
                src_ref=gram.at[rows_of(h, 1 - lo)],
                dst_ref=half.at[h],
                send_sem=d1s.at[h],
                recv_sem=d1r.at[h],
                device_id=(pole, sibling, z),
                device_id_type=MESH,
            )
        )
        halves[h].start()

    receive(chunks - 2)

    for h in range(2):
        halves[h].wait_recv()
        half_sum[h] = (gram[rows_of(h, lo)] + half[h]).reshape(zs, db, block)

    def part(j):
        return pltpu.make_async_remote_copy(
            src_ref=half_sum.at[j // zs, j % zs],
            dst_ref=parts.at[mine],
            send_sem=d2s.at[j],
            recv_sem=d2r.at[mine],
            device_id=(pole, (j // zs) * 2 + lo, j % zs),
            device_id_type=MESH,
        )

    def part_from(j):
        return pltpu.make_async_remote_copy(
            src_ref=parts.at[j],
            dst_ref=parts.at[j],
            send_sem=d2s.at[j],
            recv_sem=d2r.at[j],
            device_id=(pole, (j // zs) * 2 + lo, j % zs),
            device_id_type=MESH,
        )

    def peers(visit):
        @pl.loop(0, 2 * zs)
        def _(j):
            @pl.when(j != mine)
            def _():
                visit(j)

    peers(lambda j: part(j).start())
    parts[mine] = half_sum[hi, z]
    receive(chunks - 1)
    peers(lambda j: part_from(j).wait_recv())
    total = parts[0]
    for j in range(1, 2 * zs):
        total = total + parts[j]
    dinv = dinv_ref[...].astype(F32)
    totals[pole] = (wr * dinv[1] + wi * dinv[0]) - total

    def result(p, slot):
        return pltpu.make_async_remote_copy(
            src_ref=totals.at[slot],
            dst_ref=totals.at[slot],
            send_sem=d3s.at[p],
            recv_sem=d3r.at[slot],
            device_id=(p, row, z),
            device_id_type=MESH,
        )

    others(lambda p: result(p, pole).start())

    @pl.loop(0, chunks)
    def _(c):
        @pl.loop(0, zs)
        def _(zz):
            over(c, 0, zz).wait_send()
            over(c, 1, zz).wait_send()

            cross(c, zz).wait_send()

            along(lambda: up(c, zz).wait_send(), lambda: down(c, zz).wait_send(), zz)

        others(lambda p: share(c, p).wait_send())

    for h in range(2):
        halves[h].wait_send()
    peers(lambda j: part(j).wait_send())
    others(lambda p: result(p, p).wait_recv())
    final = totals[0]
    for p in range(1, poles):
        final = final + totals[p]
    diag_ref[...] = final
    others(lambda p: result(p, pole).wait_send())


def local(inverse, factor, diag_inverse, widths, pattern, owner, assign, pole_weights):
    zs = lax.axis_size("col")
    poles = lax.axis_size("pole")
    rows_n = lax.axis_size("row")
    assert rows_n == 4
    devices = rows_n * zs
    local_width = factor.shape[2]
    total_cols = factor.shape[3]
    db = diag_inverse.shape[2]
    block = diag_inverse.shape[3]
    blocks_k = total_cols // block
    live = 2 * total_cols // 3
    width = 128
    chunks = live // width

    dims = (chunks, zs, poles, width, blocks_k, block, db)
    vmem = pl.BlockSpec(memory_space=pltpu.VMEM)
    hbm = pl.BlockSpec(memory_space=pl.ANY)
    smem = pl.BlockSpec(memory_space=pltpu.SMEM)
    dma = pltpu.SemaphoreType.DMA
    return pl.pallas_call(
        functools.partial(kernel, dims),
        out_shape=(
            jax.ShapeDtypeStruct((local_width, total_cols), F32),
            jax.ShapeDtypeStruct((db, block), F32),
        ),
        in_specs=[hbm, hbm, vmem, smem, vmem, smem, smem, vmem],
        out_specs=(vmem, vmem),
        scratch_shapes=[
            pltpu.VMEM((2, local_width, total_cols), BF16),
            pltpu.VMEM((chunks, total_cols, width), BF16),
            pltpu.VMEM((chunks, devices, 2 * width, local_width), BF16),
            pltpu.VMEM((2, devices, local_width, local_width), BF16),
            pltpu.VMEM((chunks, 2 * width, local_width), F32),
            pltpu.VMEM((chunks, 2 * width, local_width), BF16),
            pltpu.VMEM((chunks, poles, width, local_width), F32),
            pltpu.VMEM((2, total_cols, local_width), BF16),
            pltpu.VMEM((2, total_cols, local_width), BF16),
            pltpu.VMEM((total_cols, block), F32),
            pltpu.VMEM((2, zs * db, block), F32),
            pltpu.VMEM((2, zs, db, block), F32),
            pltpu.VMEM((2 * zs, db, block), F32),
            pltpu.VMEM((poles, db, block), F32),
            dma,
            dma,
            dma((chunks, devices)),
            dma((chunks, zs, 2)),
            dma((chunks, zs)),
            dma((chunks, 2, zs)),
            dma((chunks, poles)),
            dma((chunks, poles)),
            dma((2,)),
            dma((2,)),
            dma((2 * zs,)),
            dma((2 * zs,)),
            dma((poles,)),
            dma((poles,)),
        ],
        compiler_params=pltpu.CompilerParams(
            collective_id=0, has_side_effects=True, vmem_limit_bytes=60 * 1024 * 1024
        ),
    )(
        factor[0],
        inverse[0].reshape(2, devices, local_width, local_width),
        diag_inverse[0],
        widths,
        pattern.T,
        owner,
        assign,
        pole_weights.T,
    )


def solution(mesh):
    placed = (
        P("pole", None, None, ("row", "col")),
        P("pole", None, ("row", "col"), None),
        P("pole", None, ("row", "col"), None),
        P(),
        P(),
        P(),
        P("pole"),
        P(),
    )
    return jax.shard_map(
        local,
        mesh=mesh,
        in_specs=placed,
        out_specs=(P(("row", "col"), None), P(("row", "col"), None)),
        check_vma=False,
    )
```
